256 devices in a mesh: seq: 8 (over x, core), tab: 32 (over z, y).
Axes of the slice: x: 4, y: 4, z: 8, core: 2. Of those that a mesh axis runs over, the one named last changes fastest.
Arguments:
- history_rows: bfloat16 [32, 1024, 512], P('tab', 'seq'), may hold values from -36 to 36
- out_grad: bfloat16 [32, 1024, 512], P('tab', 'seq'), may hold values from -6 to 6
- seg_lengths: int32 [32, 4], P('tab'), may hold values from 1 to 512, 1024 in all within a row
- hot_flag: int32 [32, 1024], P('tab', 'seq'), may hold values 0 or 1
- hot_slot: int32 [32, 1024], P('tab', 'seq'), may hold values from 0 to 2047
- cold_owner: int32 [32, 1024, 1], P('tab', 'seq'), may hold values from 0 to 255; in each aligned block of 128 rows (0 to 127, 128 to 255, ..., all dimensions but the last counted through in order) at most 2 rows name the same one
- cold_row: int32 [32, 1024], P('tab', 'seq'), may hold values from 0 to 511
- input_weight: bfloat16 [512, 2048], replicated, may hold values from -0.25 to 0.25
- w_out: bfloat16 [512, 512], replicated, may hold values from -0.25 to 0.25
Outputs:
- cold_grad: float32 [131072, 512], P(('seq', 'tab'))
- hot_grad: float32 [2048, 512], P('tab')
The draws below stay inside these ranges and needn't reach their ends.
Inputs may be any that keep to these rules, and one draw needn't show every extreme that they name: `seg_lengths`: each row sums to 1024, and its longest entry is exactly 512. `hot_slot`: read only where hot_flag is 1. `cold_owner`: owners are numbered with seq slowest, owner = seq index * 32 + tab index; among the 128 positions held by one device no owner is named more than 2 times, a bound that some block reaches; read only where hot_flag is 0. `cold_row`: read only where hot_flag is 0.
All inputs are finite; a program needn't handle non-finite values. No bound on the sum of `hot_flag` on one device may be relied on, other than what follows from the above.
Results may differ from the reference program's by a relative error of at most 0.012.
Values may be sent and summed in bfloat16 or wider, within the bound.
A program may use at most 64 MiB of HBM per device.

```python
import math
import jax
import jax.numpy as jnp
import numpy as np
from jax import lax

D = 512
HEADS = 8
TOK_DEV = 128
GLEN = 1024
GROUPS = 32
NSEG = 4
MOST = 512
HOT = 2048
ROWS_DEV = 512
ROWS = 131072
CAP = 2
DEVICES = 256


def draw_history_rows(key, part):
    key = jax.random.fold_in(key, 11)
    key_base, key_row, key_col = jax.random.split(key, 3)
    row_scale = jnp.exp(jax.random.uniform(key_row, (GROUPS, GLEN, 1), jnp.float32, math.log(0.3), math.log(3.0)))
    col_scale = jnp.exp(jax.random.uniform(key_col, (D,), jnp.float32, math.log(0.3), math.log(3.0)))
    base = jnp.clip(jax.random.normal(key_base, (GROUPS, GLEN, D), jnp.float32), -4.0, 4.0)
    return (base * row_scale * col_scale).astype(jnp.bfloat16)


def with_ends(drawn, own_key, low, largest):
    index_at = [jax.random.randint(jax.random.fold_in(own_key, axis), (), 0, length) for axis, length in enumerate(drawn.shape)]
    longest = drawn.shape.index(max(drawn.shape))
    beside = index_at[:longest] + [(index_at[longest] + 1) % drawn.shape[longest]] + index_at[longest + 1:]
    return drawn.at[tuple(index_at)].set(low).at[tuple(beside)].set(largest)


def block_scale(rng, extent, cuts, least, top_value):
    def one(position, blocks):
        draws = jax.random.uniform(jax.random.fold_in(jax.random.fold_in(rng, 6), position), (blocks,), jnp.float32, least / len(cuts), top_value / len(cuts))
        return jnp.repeat(jnp.exp(draws), extent[position] // blocks).reshape((-1,) + (1,) * (len(extent) - position - 1))

    level = one(*cuts[0])
    for cut in cuts[1:]:
        level = level * one(*cut)
    return level


def rank_table(number_of, slope):
    weights = [(1 << 20) // math.isqrt(grade ** slope) + 1 for grade in range(1, number_of + 1)]
    scale = 1 + sum(weights) // (1 << 30)
    return np.cumsum(np.array([max(1, weight // scale) for weight in weights]))


def skewed_ids(own_key, dims, count, slope):
    grid = rank_table(count, slope)
    ticket = jax.random.randint(jax.random.fold_in(own_key, 1), dims, 0, int(grid[count - 1]))
    grade = jnp.searchsorted(jnp.asarray(grid, jnp.int32), ticket, side="right")
    return jax.random.permutation(jax.random.fold_in(own_key, 2), count)[grade].astype(jnp.int32)


def profile(number_of, total, limit, slope):
    loads = [(1 << 20) // math.isqrt(grade ** slope) + 1 for grade in range(2, number_of + 1)]
    spare, given = total - limit - (number_of - 1), [1] * (number_of - 1)
    while spare > 0:
        candidates = [i for i in range(number_of - 1) if given[i] < limit]
        mass, budget = sum([loads[i] for i in candidates]), spare
        for i in candidates:
            addition = min(limit - given[i], max(1, budget * loads[i] // mass), spare)
            given[i] = given[i] + addition
            spare = spare - addition
    return np.array([limit] + given)


def ragged(rng, number_of, total, reach, lean):
    if number_of == 2:
        one = jax.random.randint(rng, (), max(1, total - reach), min(reach, total - 1) + 1)
        return jnp.stack([one, total - one])
    sizes = jnp.asarray(profile(number_of, total, reach, lean), jnp.int32)
    couples = (number_of - 1) // 2
    giver, taker = sizes[1:1 + 2 * couples:2], sizes[2:2 + 2 * couples:2]
    slack = jnp.minimum(giver - 1, reach - taker)
    moved = jax.random.randint(jax.random.fold_in(rng, 1), (couples,), 0, 1 << 20) % (slack + 1)
    sizes = sizes.at[1:1 + 2 * couples:2].set(giver - moved).at[2:2 + 2 * couples:2].set(taker + moved)
    return sizes[jax.random.permutation(jax.random.fold_in(rng, 2), number_of)]


def routed_block(own_key, own, number, rows, count, top, reach, slope):
    ranking = jax.random.permutation(own_key, count)
    packed, usual = load_shares(count, rows * top, reach, slope, True), load_shares(count, rows * top, reach, slope, False)
    places = jnp.arange(count)

    def named(sizes, offset_by):
        used = int((sizes > 0).sum())
        fixed = max(1, used // 4)
        shifted = fixed + (places - fixed + offset_by * (used - fixed)) % max(1, count - fixed)
        return jnp.zeros((count,), jnp.int32).at[ranking[jnp.where(places < fixed, places, shifted)]].set(jnp.asarray(sizes, jnp.int32))

    sizes = jnp.where(number % 4 == 0, named(packed, number // 4), named(usual, number - number // 4 - 1))
    mixed = jax.random.permutation(jax.random.fold_in(own, 3), count)
    source_of, receiver = mixed[0:count // 2 * 2:2], mixed[1:count // 2 * 2:2]
    room = jnp.minimum(sizes[source_of] - 1, reach - sizes[receiver]) // 2
    room = jnp.where((source_of == ranking[0]) | (receiver == ranking[0]) | (sizes[receiver] == 0), 0, jnp.maximum(room, 0))
    shifted = jax.random.randint(jax.random.fold_in(own, 4), (count // 2,), 0, 1 << 20) % (room + 1)
    sizes = sizes.at[source_of].add(-shifted).at[receiver].add(shifted)
    items = jnp.searchsorted(jnp.cumsum(sizes), jnp.arange(rows * top), side="right").astype(jnp.int32)
    grid = items.reshape(top, rows).T
    grid = grid[jax.random.permutation(jax.random.fold_in(own, 1), rows)]
    offset_by = jax.random.randint(jax.random.fold_in(own, 2), (rows, 1), 0, top)
    return jnp.take_along_axis(grid, (jnp.arange(top)[None, :] + offset_by) % top, axis=1)


def load_shares(amount, total, most, lean, full):
    weights = [(1 << 20) // math.isqrt(grade ** lean) + 1 for grade in range(1, amount + 1)]
    largest = most if full else min(most, max(-(-total // amount), total * weights[0] // sum(weights)))
    least = 1 if total - largest >= amount - 1 else 0
    holding, surplus = [largest] + [least] * (amount - 1), total - largest - least * (amount - 1)
    while surplus > 0:
        candidates = [i for i in range(1, amount) if holding[i] < largest] or [i for i in range(1, amount) if holding[i] < most]
        whole, left = sum([weights[i] for i in candidates]), surplus
        for i in candidates:
            extra = min(most - holding[i], max(1, left * weights[i] // whole), surplus)
            holding[i] = holding[i] + extra
            surplus = surplus - extra
    return np.array(holding)


def scatter_about(stream_key, extent, width, limit, shards=(), held_as=jnp.bfloat16):
    gain = block_scale(stream_key, extent, shards, -0.22, 0.18) if shards else 1.0
    array = jax.random.normal(stream_key, extent, jnp.float32) * width * gain
    return jnp.minimum(jnp.maximum(array, -limit), limit).astype(held_as)


def setup_inputs(seed: int = 0) -> dict:
    key_list = jax.random.split(jax.random.key(seed), 10)
    history_rows = draw_history_rows(jax.random.fold_in(key_list[9], 71), 0)
    out_grad = scatter_about(key_list[1], (GROUPS, GLEN, D), 1.0, 6.0, ((0, 32), (1, 8)))
    seg_lengths = jax.vmap(lambda own: ragged(own, NSEG, GLEN, MOST, 2))(jax.random.split(key_list[2], GROUPS)).reshape((GROUPS, NSEG)).astype(jnp.int32)
    hot_flag = with_ends((jax.random.randint(key_list[3], (GROUPS, GLEN), 0, 5) < 1).astype(jnp.int32), jax.random.fold_in(key_list[3], 1), 0, 1)
    hot_slot = with_ends(skewed_ids(key_list[4], (GROUPS, GLEN), HOT, 1), jax.random.fold_in(key_list[4], 3), 0, HOT - 1).astype(jnp.int32)
    cold_owner_keys = jax.random.split(jax.random.fold_in(key_list[5], 1), GROUPS * GLEN // TOK_DEV)
    cold_owner_turns = jax.random.permutation(jax.random.fold_in(key_list[5], 3), GROUPS * GLEN // TOK_DEV)
    cold_owner = jax.vmap(lambda own, number: routed_block(jax.random.fold_in(key_list[5], 2), own, number, TOK_DEV, DEVICES, 1, CAP, 1))(cold_owner_keys, cold_owner_turns).reshape((GROUPS, GLEN, 1))
    cold_row = with_ends(jax.random.randint(key_list[6], (GROUPS, GLEN), 0, ROWS_DEV), jax.random.fold_in(key_list[6], 1), 0, ROWS_DEV - 1).astype(jnp.int32)
    input_weight = scatter_about(key_list[7], (D, 4 * D), D ** -0.5, 0.25)
    w_out = scatter_about(key_list[8], (D, D), D ** -0.5, 0.25)
    return {"history_rows": history_rows, "out_grad": out_grad, "seg_lengths": seg_lengths, "hot_flag": hot_flag, "hot_slot": hot_slot, "cold_owner": cold_owner, "cold_row": cold_row, "input_weight": input_weight, "w_out": w_out}


EPS = 1e-05

def swish_slope(value):
    sigma = jax.nn.sigmoid(value)
    return sigma * (1.0 + value * (1.0 - sigma))

def layer_norm_reverse(grad, normed, inv_scale):
    return inv_scale * (grad - lax.optimization_barrier(jnp.mean(grad, axis=1, keepdims=True)) - normed * lax.optimization_barrier(jnp.mean(grad * normed, axis=1, keepdims=True)))

def group_grad(rows_in, incoming_gradient, lengths, input_weight, w_out):
    group_len, model_width = rows_in.shape
    head_dim = model_width // HEADS
    score_scale = head_dim ** (-0.5)
    rows_wide = rows_in.astype(jnp.float32)
    centered_input = rows_wide - lax.optimization_barrier(jnp.mean(rows_wide, axis=1, keepdims=True))
    inverse_deviation = lax.rsqrt(lax.optimization_barrier(jnp.mean(centered_input * centered_input, axis=1, keepdims=True)) + EPS)
    normalized_input = centered_input * inverse_deviation
    projected_input = jnp.dot(normalized_input.astype(jnp.bfloat16), input_weight, preferred_element_type=jnp.float32)
    hidden = jax.nn.silu(projected_input).astype(jnp.bfloat16)
    gate_up = hidden[:, :model_width]
    values = hidden[:, model_width:2 * model_width].astype(jnp.float32)
    queries = hidden[:, 2 * model_width:3 * model_width].astype(jnp.float32)
    key_rows = hidden[:, 3 * model_width:].astype(jnp.float32)
    seg_ends = jnp.cumsum(lengths)
    positions = jnp.arange(group_len, dtype=jnp.int32)
    key_seg = lax.optimization_barrier(jnp.sum((positions[:, None] >= seg_ends[None, :]).astype(jnp.int32), axis=1))
    key_heads = key_rows.reshape(group_len, HEADS, head_dim)
    value_heads = values.reshape(group_len, HEADS, head_dim)
    blocks = group_len // TOK_DEV

    def block_grad(running, block_index):
        offset = (block_index * TOK_DEV).astype(jnp.int32)
        query_heads = lax.dynamic_slice_in_dim(queries, offset, TOK_DEV, 0).reshape(TOK_DEV, HEADS, head_dim)
        gate_block = lax.dynamic_slice_in_dim(gate_up, offset, TOK_DEV, 0).astype(jnp.float32)
        grad_block = lax.dynamic_slice_in_dim(incoming_gradient, offset, TOK_DEV, 0)
        query_pos = offset + jnp.arange(TOK_DEV, dtype=jnp.int32)
        query_seg = lax.dynamic_slice_in_dim(key_seg, offset, TOK_DEV, 0)
        allowed = (query_seg[:, None] == key_seg[None, :]) & (positions[None, :] <= query_pos[:, None])
        scores = jnp.einsum('thd,khd->htk', query_heads, key_heads) * score_scale
        weights = jnp.where(allowed[None], jax.nn.silu(scores), 0.0).astype(jnp.bfloat16).astype(jnp.float32)
        attended = jnp.einsum('htk,khd->thd', weights, value_heads).reshape(TOK_DEV, model_width)
        mixed_centred = attended - lax.optimization_barrier(jnp.mean(attended, axis=1, keepdims=True))
        inv_mixed = lax.rsqrt(lax.optimization_barrier(jnp.mean(mixed_centred * mixed_centred, axis=1, keepdims=True)) + EPS)
        mixed_norm = mixed_centred * inv_mixed
        grad_gated = jnp.dot(grad_block, w_out.T, preferred_element_type=jnp.float32)
        grad_gate = grad_gated * mixed_norm
        grad_mixed = layer_norm_reverse(grad_gated * gate_block, mixed_norm, inv_mixed).astype(jnp.bfloat16).astype(jnp.float32)
        grad_heads = grad_mixed.reshape(TOK_DEV, HEADS, head_dim)
        grad_weights = jnp.einsum('thd,khd->htk', grad_heads, value_heads)
        grad_scores = jnp.where(allowed[None], grad_weights * swish_slope(scores) * score_scale, 0.0).astype(jnp.bfloat16).astype(jnp.float32)
        grad_query = jnp.einsum('htk,khd->thd', grad_scores, key_heads).reshape(TOK_DEV, model_width)
        value_part = jnp.einsum('htk,thd->khd', weights, grad_heads).reshape(group_len, model_width)
        key_part = jnp.einsum('htk,thd->khd', grad_scores, query_heads).reshape(group_len, model_width)
        key_terms = lax.optimization_barrier(jnp.concatenate([value_part, key_part], axis=1).astype(jnp.bfloat16)).astype(jnp.float32)
        return (running + key_terms, (grad_gate, grad_query))
    start_terms = jnp.zeros((group_len, 2 * model_width), jnp.float32)
    key_grads, (grad_gate, grad_query) = lax.scan(block_grad, start_terms, jnp.arange(blocks, dtype=jnp.int32))
    grad_gate = grad_gate.reshape(group_len, model_width)
    grad_query = grad_query.reshape(group_len, model_width)
    grad_hidden = jnp.concatenate([grad_gate, key_grads[:, :model_width], grad_query, key_grads[:, model_width:]], axis=1)
    grad_proj = (grad_hidden * swish_slope(projected_input)).astype(jnp.bfloat16)
    input_gradient = jnp.dot(grad_proj, input_weight.T, preferred_element_type=jnp.float32)
    return incoming_gradient.astype(jnp.float32) + layer_norm_reverse(input_gradient, normalized_input, inverse_deviation)

def reference(history_rows, out_grad, seg_lengths, hot_flag, hot_slot, cold_owner, cold_row, input_weight, w_out):
    row_gradients = lax.map(lambda members: group_grad(members[0], members[1], members[2], input_weight, w_out), (history_rows, out_grad, seg_lengths))
    flat_rows = row_gradients.reshape(GROUPS * GLEN, D)
    is_hot = hot_flag.reshape(-1) == 1
    hot_values = jnp.where(is_hot[:, None], flat_rows, 0.0)
    hot_grad = jnp.zeros((HOT, D), jnp.float32).at[hot_slot.reshape(-1).astype(jnp.int32)].add(hot_values)
    rounded = lax.optimization_barrier(flat_rows.astype(jnp.bfloat16)).astype(jnp.float32)
    cold_values = jnp.where(is_hot[:, None], 0.0, rounded)
    targets = (cold_owner.reshape(-1) * ROWS_DEV + cold_row.reshape(-1)).astype(jnp.int32)
    cold_grad = jnp.zeros((ROWS, D), jnp.float32).at[targets].add(cold_values)
    return (cold_grad, hot_grad)
```

```python
import functools

import jax
import jax.numpy as jnp
from jax import lax
from jax.experimental import pallas as pl
from jax.experimental.pallas import tpu as pltpu
from jax.sharding import PartitionSpec as P

HEADS = 8
HEAD = 64
LEN = 128
WIDTH = 512
BAND = 4
EPS = 1e-05
MESH = pl.DeviceIdType.MESH
F32 = jnp.float32
BF16 = jnp.bfloat16
I32 = jnp.int32
VALUE, QUERY, KEY = 0, 1, 2
GATE, GATED = 0, 1


def mm(a, b):
    return jnp.dot(a, b, preferred_element_type=F32)


def mm_t(a, b):
    return lax.dot_general(a, b, (((1,), (1,)), ((), ())), preferred_element_type=F32)


def sigmoid(v):
    return 0.5 * jnp.tanh(0.5 * v) + 0.5


def iota(shape, dim):
    return lax.broadcasted_iota(I32, shape, dim)


def kernel(
    seqs, tabs,
    x_ref, og_ref, seg_ref, flag_ref, slot_ref, owner_ref, row_ref, w_ref, wo_ref,
    cold_ref, hot_ref,
    qkv_send, qkv_recv, gg_send, gg_recv, id_send, id_recv, stat_send, stat_recv, ggr_send, ggr_recv, dg_send, dg_recv,
    row_send, row_recv, cold_send, cold_recv, tab_send, tab_recv, num_send, num_recv, hot_send, hot_recv, sum_send, sum_recv,
    proj, slope_in, xhat, keys, values, weight, slope, att, dkv, gproj, hits, own_hits,
    qkv_ss, qkv_rs, gg_ss, gg_rs, id_ss, id_rs, stat_ss, stat_rs, ggr_ss, ggr_rs, dg_ss, dg_rs,
    row_ss, row_rs, cold_ss, cold_rs, tab_ss, tab_rs, num_ss, num_rs, hot_ss, hot_rs, sum_ss, sum_rs,
):
    me = lax.axis_index("seq")
    tab = lax.axis_index("tab")
    chunks = cold_send.shape[1]
    lanes = tabs // chunks
    share = 64

    def to_seq(src, dst, ss, rs, peer):
        return pltpu.make_async_remote_copy(
            src_ref=src, dst_ref=dst, send_sem=ss, recv_sem=rs, device_id={"seq": peer}, device_id_type=MESH
        )

    def to_tab(src, dst, ss, rs, peer):
        return pltpu.make_async_remote_copy(
            src_ref=src, dst_ref=dst, send_sem=ss, recv_sem=rs, device_id={"tab": peer}, device_id_type=MESH
        )

    def got_seq(slot, ss, rs, source):
        @pl.when(source != me)
        def _():
            to_seq(slot, slot, ss, rs, source).wait_recv()

    def got_tab(slot, ss, rs, source):
        @pl.when(source != tab)
        def _():
            to_tab(slot, slot, ss, rs, source).wait_recv()

    barrier = pltpu.get_barrier_semaphore()
    for step in range(1, seqs):
        pl.semaphore_signal(barrier, inc=1, device_id={"seq": lax.rem(me + step, seqs)}, device_id_type=MESH)

    @pl.loop(1, tabs)
    def _(step):
        pl.semaphore_signal(barrier, inc=1, device_id={"tab": lax.rem(tab + step, tabs)}, device_id_type=MESH)

    wide = x_ref[...].astype(F32)
    centered = wide - jnp.mean(wide, axis=1, keepdims=True)
    normed = centered * lax.rsqrt(jnp.mean(centered * centered, axis=1, keepdims=True) + EPS)
    xin = normed.astype(BF16)

    def project(block, pair):
        at = pl.multiple_of(block * WIDTH + pair * LEN, LEN)
        out = mm(xin, w_ref[:, pl.ds(at, LEN)]).T
        proj[pl.ds(at, LEN), :] = out
        return (out * sigmoid(out)).astype(BF16).reshape(2, HEAD, LEN)

    for step in range(HEADS // 2):
        pair = lax.rem(me // 2 + 1 + step, HEADS // 2)
        for part, block in ((VALUE, 1), (QUERY, 2), (KEY, 3)):
            qkv_send[pl.ds(2 * pair, 2), part] = project(block, pair)
        if step == 0:
            pl.semaphore_wait(barrier, seqs - 1 + tabs - 1)
        for core in range(2):
            peer = 2 * pair + core

            @pl.when(peer != me)
            def _():
                to_seq(qkv_send.at[peer], qkv_recv.at[me], qkv_ss.at[peer], qkv_rs.at[me], peer).start()

    qkv_recv[me] = qkv_send[me]

    flag = flag_ref[...]
    owner = jnp.where(flag == 1, -1, owner_ref[...])
    owner_row = jnp.broadcast_to(owner.astype(F32), (LEN, LEN))
    earlier = (owner_row.T == owner_row) & (iota((LEN, LEN), 0) < iota((LEN, LEN), 1))
    taken = jnp.sum(jnp.where(earlier, 1.0, 0.0), axis=0, keepdims=True)
    lane_of = jnp.where(flag == 1, -1, owner * 2 + taken.astype(I32))
    which = iota((8, LEN), 0)
    id_send[...] = jnp.where(
        which == 0,
        jnp.where(flag == 1, slot_ref[...], -1),
        jnp.where(which == 1, lane_of, jnp.where(which == 2, row_ref[...], 0)),
    )
    for step in range(1, seqs):
        peer = lax.rem(me + step, seqs)
        to_seq(id_send, id_recv.at[me], id_ss.at[peer], id_rs.at[me], peer).start()
    id_recv[me] = id_send[...]

    for step in range(HEADS // 2):
        pair = lax.rem(me // 2 + 1 + step, HEADS // 2)
        at = pl.multiple_of(pair * LEN, LEN)
        gg_send[pl.ds(2 * pair, 2), GATE] = project(0, pair)
        gg_send[pl.ds(2 * pair, 2), GATED] = mm_t(wo_ref[pl.ds(at, LEN), :], og_ref[...]).astype(BF16).reshape(2, HEAD, LEN)
        for core in range(2):
            peer = 2 * pair + core

            @pl.when(peer != me)
            def _():
                to_seq(gg_send.at[peer], gg_recv.at[me], gg_ss.at[peer], gg_rs.at[me], peer).start()

    gg_recv[me] = gg_send[me]

    end0 = seg_ref[0, 0]
    end1 = end0 + seg_ref[0, 1]
    end2 = end1 + seg_ref[0, 2]
    for block in range(seqs):
        low = max(0, block - BAND)
        count = block + 1 - low
        got_seq(qkv_recv.at[block], qkv_ss.at[block], qkv_rs.at[block], block)
        keys[pl.ds(block * LEN, LEN), :] = qkv_recv[block, KEY].astype(F32).T.astype(BF16)
        values[pl.ds(block * LEN, LEN), :] = qkv_recv[block, VALUE].astype(F32).T.astype(BF16)
        score = mm(keys[pl.ds(low * LEN, count * LEN), :], qkv_recv[block, QUERY]) * 0.125
        here = block * LEN + iota((1, LEN), 1)
        start = jnp.where(here >= end2, end2, jnp.where(here >= end1, end1, jnp.where(here >= end0, end0, 0)))
        there = low * LEN + iota(score.shape, 0)
        allowed = (there >= start) & (there <= here)
        gate = sigmoid(score)
        swish = score * gate
        heavy = jnp.where(allowed, swish, 0.0).astype(BF16)
        weight[block, pl.ds(0, count * LEN), :] = heavy
        slope[block, pl.ds(0, count * LEN), :] = jnp.where(allowed, (gate + swish * (1.0 - gate)) * 0.125, 0.0)
        across = jnp.concatenate([qkv_recv[other, VALUE] for other in range(low, block + 1)], axis=1)
        mixed = mm(across, heavy)
        att[block] = mixed
        got_seq(gg_recv.at[block], gg_ss.at[block], gg_rs.at[block], block)
        grad = gg_recv[block, GATE].astype(F32) * gg_recv[block, GATED].astype(F32)
        mean = jnp.mean(mixed, axis=0, keepdims=True)
        off = mixed - mean
        stat_send[0, pl.ds(block, 1), :] = mean
        stat_send[1, pl.ds(block, 1), :] = jnp.sum(off * off, axis=0, keepdims=True)
        stat_send[2, pl.ds(block, 1), :] = jnp.sum(grad, axis=0, keepdims=True)
        stat_send[3, pl.ds(block, 1), :] = jnp.sum(grad * off, axis=0, keepdims=True)

    for step in range(1, seqs):
        peer = lax.rem(me + step, seqs)
        to_seq(stat_send, stat_recv.at[me], stat_ss.at[peer], stat_rs.at[me], peer).start()
    stat_recv[me] = stat_send[...]

    for source in range(seqs):
        got_seq(id_recv.at[source], id_ss.at[source], id_rs.at[source], source)
    passed = num_send.shape[0] * num_send.shape[1]
    place = iota((passed, LEN), 0)
    numbers = jnp.zeros((passed, LEN), F32)
    for source in range(seqs):
        wanted = jnp.where(
            lax.rem(place, 2 * seqs) // 2 == source,
            (me * tabs + place // (2 * seqs)) * 2 + lax.rem(place, 2),
            -5,
        )
        pick = jnp.where(wanted == id_recv[source, 1:2, :], 1.0, 0.0).astype(BF16)
        number = id_recv[source, 2:3, :]
        line = iota((LEN, LEN), 0)
        halves = jnp.where(line == 0, number >> 4, jnp.where(line == 1, number & 15, 0))
        numbers = numbers + mm_t(pick, halves.astype(F32).astype(BF16))
    num_send[...] = numbers.astype(BF16).reshape(num_send.shape)

    @pl.loop(1, tabs)
    def _(step):
        peer = lax.rem(tab + step, tabs)
        to_tab(num_send.at[peer], num_recv.at[tab], num_ss.at[peer], num_rs.at[tab], peer).start()

    num_recv[tab] = num_send[tab]

    for source in range(seqs):
        got_seq(stat_recv.at[source], stat_ss.at[source], stat_rs.at[source], source)
    means = [stat_recv[source, 0] for source in range(seqs)]
    mean = sum(means) * (1.0 / seqs)
    spread = sum(stat_recv[source, 1] + HEAD * (means[source] - mean) ** 2 for source in range(seqs))
    inv = lax.rsqrt(spread * (1.0 / WIDTH) + EPS)
    first = sum(stat_recv[source, 2] for source in range(seqs)) * (1.0 / WIDTH)
    second = sum(stat_recv[source, 3] + (means[source] - mean) * stat_recv[source, 2] for source in range(seqs))
    second = inv * second * (1.0 / WIDTH)

    for block in range(seqs):
        def line(array):
            return array[block : block + 1, :]

        gated = gg_recv[block, GATED].astype(F32)
        normed_here = (att[block] - line(mean)) * line(inv)
        ggr_send[block] = (gated * normed_here).astype(BF16)
        att[block] = line(inv) * (gg_recv[block, GATE].astype(F32) * gated - line(first) - normed_here * line(second))

    for step in range(1, seqs):
        peer = lax.rem(me + step, seqs)
        to_seq(ggr_send.at[peer], ggr_recv.at[me], ggr_ss.at[peer], ggr_rs.at[me], peer).start()
    ggr_recv[me] = ggr_send[me]

    for block in reversed(range(seqs)):
        low = max(0, block - BAND)
        count = block + 1 - low
        grad = att[block].astype(BF16)
        query = qkv_recv[block, QUERY]
        span = pl.ds(low * LEN, count * LEN)
        grad_weight = mm(values[span, :], grad)
        grad_score = (grad_weight * slope[block, pl.ds(0, count * LEN), :]).astype(BF16)
        across = jnp.concatenate([qkv_recv[other, KEY] for other in range(low, block + 1)], axis=1)
        grad_value = mm_t(grad, weight[block, pl.ds(0, count * LEN), :])
        grad_key = mm_t(query, grad_score)
        dg_send[block, QUERY] = mm(across, grad_score).astype(BF16)
        for other in range(low, block + 1):
            cut = slice((other - low) * LEN, (other - low + 1) * LEN)
            new_value, new_key = grad_value[:, cut], grad_key[:, cut]
            if block < min(seqs - 1, other + BAND):
                new_value, new_key = new_value + dkv[other, 0], new_key + dkv[other, 1]
            if other == block:
                dg_send[block, VALUE] = new_value.astype(BF16)
                dg_send[block, KEY] = new_key.astype(BF16)
            else:
                dkv[other, 0] = new_value
                dkv[other, 1] = new_key

        @pl.when(block != me)
        def _():
            to_seq(dg_send.at[block], dg_recv.at[me], dg_ss.at[block], dg_rs.at[me], block).start()

    dg_recv[me] = dg_send[me]

    across = x_ref[...].astype(F32).T
    across = across - jnp.mean(across, axis=0, keepdims=True)
    inv_in = lax.rsqrt(jnp.mean(across * across, axis=0, keepdims=True) + EPS)
    xhat[...] = across * inv_in

    @pl.loop(0, 4)
    def _(block):
        span = pl.ds(pl.multiple_of(block * WIDTH, WIDTH), WIDTH)
        value = proj[span, :]
        gate = sigmoid(value)
        slope_in[span, :] = gate * (1.0 + value * (1.0 - gate))

    hot_ids = jnp.concatenate([id_recv[source, 0:1, :] for source in range(seqs)], axis=1)

    @pl.loop(0, hits.shape[0] // LEN)
    def _(block):
        at = pl.multiple_of(block * LEN, LEN)
        hits[pl.ds(at, LEN), :] = jnp.where(iota((LEN, seqs * LEN), 0) + at == hot_ids, 1.0, 0.0).astype(BF16)

    own_lanes = id_send[1:2, :]
    own_hits[...] = jnp.where(iota(own_hits.shape, 0) == own_lanes, 1.0, 0.0).astype(BF16)

    for source in range(seqs):
        got_seq(ggr_recv.at[source], ggr_ss.at[source], ggr_rs.at[source], source)
        at = source * HEAD
        gproj[pl.ds(at, HEAD), :] = (ggr_recv[source].astype(F32) * slope_in[pl.ds(at, HEAD), :]).astype(BF16)
    grad_in = mm(w_ref[:, 0:WIDTH], gproj[0:WIDTH, :])
    for source in reversed(range(seqs)):
        got_seq(dg_recv.at[source], dg_ss.at[source], dg_rs.at[source], source)
        for part in range(3):
            at = (part + 1) * WIDTH + source * HEAD
            gproj[pl.ds(at, HEAD), :] = (dg_recv[source, part].astype(F32) * slope_in[pl.ds(at, HEAD), :]).astype(BF16)
    grad_in = grad_in + mm(w_ref[:, WIDTH:], gproj[WIDTH:, :])
    norm_in = xhat[...]
    grad_rows = og_ref[...].astype(F32).T + inv_in * (
        grad_in
        - jnp.mean(grad_in, axis=0, keepdims=True)
        - norm_in * jnp.mean(grad_in * norm_in, axis=0, keepdims=True)
    )
    grad_rows = grad_rows.astype(BF16)

    row_send[...] = grad_rows.reshape(row_send.shape)
    for step in range(1, seqs):
        peer = lax.rem(me + step, seqs)
        to_seq(row_send.at[peer], row_recv.at[me], row_ss.at[peer], row_rs.at[me], peer).start()
    row_recv[me] = row_send[me]

    slots = mm_t(own_hits[...], grad_rows)
    cold_send[...] = slots.astype(BF16).reshape(cold_send.shape)
    first_chunk = tab // lanes
    for turn in range(chunks):
        chunk = lax.rem(first_chunk + 1 + turn, chunks)
        for step in range(1, seqs):
            peer = lax.rem(me + step, seqs)
            to_seq(
                cold_send.at[peer, chunk], cold_recv.at[chunk, me], cold_ss.at[chunk, peer], cold_rs.at[chunk, me], peer
            ).start()
    for chunk in range(chunks):
        cold_recv[chunk, me] = cold_send[me, chunk]

    for source in range(seqs):
        got_seq(row_recv.at[source], row_ss.at[source], row_rs.at[source], source)
    slab = jnp.concatenate([row_recv[source] for source in range(seqs)], axis=1)
    left = iota((HEAD // 2, LEN), 1) < share
    for turn in range(chunks):
        chunk = lax.rem(first_chunk + 1 + turn, chunks)
        at = pl.multiple_of(chunk * lanes * share, lanes * share)
        sums = mm_t(slab, hits[pl.ds(at, lanes * share), :])
        for two in range(lanes // 2):
            both = sums[:, two * LEN : (two + 1) * LEN]
            upper, lower = both[: HEAD // 2], both[HEAD // 2 :]
            hot_send[chunk * lanes + 2 * two] = jnp.where(left, upper, pltpu.roll(lower, share, 1)).astype(BF16)
            hot_send[chunk * lanes + 2 * two + 1] = jnp.where(left, pltpu.roll(upper, share, 1), lower).astype(BF16)

        @pl.loop(0, lanes)
        def _(lane):
            peer = chunk * lanes + lane

            @pl.when(peer != tab)
            def _():
                to_tab(hot_send.at[peer], hot_recv.at[tab], hot_ss.at[peer], hot_rs.at[tab], peer).start()

    hot_recv[tab] = hot_send[tab]

    per = 2 * lanes
    out_at, in_at = iota((seqs * per, seqs * per), 0), iota((seqs * per, seqs * per), 1)
    moved = (
        (out_at // (2 * seqs) == lax.rem(in_at, per) // 2)
        & (lax.rem(out_at, 2 * seqs) // 2 == in_at // per)
        & (lax.rem(out_at, 2) == lax.rem(in_at, 2))
    )
    order = jnp.where(moved, 1.0, 0.0).astype(BF16)
    for turn in range(chunks):
        chunk = lax.rem(first_chunk + 1 + turn, chunks)
        for source in range(seqs):
            got_seq(cold_recv.at[chunk, source], cold_ss.at[chunk, source], cold_rs.at[chunk, source], source)
        rows = mm(order, cold_recv[chunk].reshape(seqs * per, WIDTH)).astype(BF16)
        tab_send[pl.ds(chunk * lanes, lanes)] = rows.reshape(lanes, 2 * seqs, WIDTH)

        @pl.loop(0, lanes)
        def _(lane):
            peer = chunk * lanes + lane

            @pl.when(peer != tab)
            def _():
                to_tab(tab_send.at[peer], tab_recv.at[tab], tab_ss.at[peer], tab_rs.at[tab], peer).start()

    tab_recv[tab] = tab_send[tab]

    @pl.loop(0, tabs)
    def _(source):
        got_tab(hot_recv.at[source], hot_ss.at[source], hot_rs.at[source], source)

    total = jnp.zeros((HEAD // 2, LEN), F32)
    for source in range(tabs):
        total = total + hot_recv[source].astype(F32)
    sum_send[...] = total
    for step in range(1, seqs):
        peer = lax.rem(me + step, seqs)
        to_seq(sum_send, sum_recv.at[me], sum_ss.at[peer], sum_rs.at[me], peer).start()
    sum_recv[me] = sum_send[...]

    @pl.loop(0, tabs)
    def _(source):
        got_tab(num_recv.at[source], num_ss.at[source], num_rs.at[source], source)

    count = 2 * seqs * tabs
    line, column = iota((8, LEN), 0), iota((8, LEN), 1)
    scale = jnp.where(line == 0, jnp.where(column == 0, 16.0, jnp.where(column == 1, 1.0, 0.0)), 0.0).astype(BF16)
    numbers = mm_t(scale, num_recv[...].reshape(count, LEN))[0:1, :].astype(I32)
    table = jnp.where(iota((cold_ref.shape[0], count), 0) == numbers, 1.0, 0.0).astype(BF16)

    @pl.loop(0, tabs)
    def _(source):
        got_tab(tab_recv.at[source], tab_ss.at[source], tab_rs.at[source], source)

    cold_ref[...] = mm(table, tab_recv[...].reshape(count, WIDTH))

    for source in range(seqs):
        got_seq(sum_recv.at[source], sum_ss.at[source], sum_rs.at[source], source)
    stacked = []
    for source in range(seqs):
        piece = sum_recv[source]
        stacked += [piece, pltpu.roll(piece, share, 1)]
    hot_ref[...] = jnp.concatenate(stacked, axis=0).T[:share, :]

    for step in range(1, seqs):
        peer = lax.rem(me + step, seqs)
        to_seq(qkv_send.at[peer], qkv_recv.at[me], qkv_ss.at[peer], qkv_rs.at[me], peer).wait_send()
        to_seq(id_send, id_recv.at[me], id_ss.at[peer], id_rs.at[me], peer).wait_send()
        to_seq(gg_send.at[peer], gg_recv.at[me], gg_ss.at[peer], gg_rs.at[me], peer).wait_send()
        to_seq(stat_send, stat_recv.at[me], stat_ss.at[peer], stat_rs.at[me], peer).wait_send()
        to_seq(ggr_send.at[peer], ggr_recv.at[me], ggr_ss.at[peer], ggr_rs.at[me], peer).wait_send()
        to_seq(dg_send.at[peer], dg_recv.at[me], dg_ss.at[peer], dg_rs.at[me], peer).wait_send()
        to_seq(row_send.at[peer], row_recv.at[me], row_ss.at[peer], row_rs.at[me], peer).wait_send()
        to_seq(sum_send, sum_recv.at[me], sum_ss.at[peer], sum_rs.at[me], peer).wait_send()
        for chunk in range(chunks):
            to_seq(
                cold_send.at[peer, chunk], cold_recv.at[chunk, me], cold_ss.at[chunk, peer], cold_rs.at[chunk, me], peer
            ).wait_send()

    @pl.loop(1, tabs)
    def _(step):
        peer = lax.rem(tab + step, tabs)
        to_tab(num_send.at[peer], num_recv.at[tab], num_ss.at[peer], num_rs.at[tab], peer).wait_send()
        to_tab(hot_send.at[peer], hot_recv.at[tab], hot_ss.at[peer], hot_rs.at[tab], peer).wait_send()
        to_tab(tab_send.at[peer], tab_recv.at[tab], tab_ss.at[peer], tab_rs.at[tab], peer).wait_send()


def solution(mesh):
    seqs, tabs = mesh.shape["seq"], mesh.shape["tab"]
    chunks = min(4, tabs // 2)
    lanes = tabs // chunks
    group = seqs * LEN

    def both(*shape):
        return [shape, shape]

    pairs = [
        ((HEADS, 3, HEAD, LEN), (seqs, 3, HEAD, LEN), BF16, (seqs,)),
        ((HEADS, 2, HEAD, LEN), (seqs, 2, HEAD, LEN), BF16, (seqs,)),
        ((8, LEN), (seqs, 8, LEN), I32, (seqs,)),
        ((4, 8, LEN), (seqs, 4, 8, LEN), F32, (seqs,)),
        ((seqs, HEAD, LEN), (HEADS, HEAD, LEN), BF16, (seqs,)),
        ((seqs, 3, HEAD, LEN), (HEADS, 3, HEAD, LEN), BF16, (seqs,)),
        ((seqs, HEAD, LEN), (seqs, HEAD, LEN), BF16, (seqs,)),
        ((seqs, chunks, 2 * lanes, WIDTH), (chunks, seqs, 2 * lanes, WIDTH), BF16, (chunks, seqs)),
        ((tabs, 2 * seqs, WIDTH), (tabs, 2 * seqs, WIDTH), BF16, (tabs,)),
        ((tabs, 2 * seqs, LEN), (tabs, 2 * seqs, LEN), BF16, (tabs,)),
        ((tabs, HEAD // 2, LEN), (tabs, HEAD // 2, LEN), BF16, (tabs,)),
        ((HEAD // 2, LEN), (seqs, HEAD // 2, LEN), F32, (seqs,)),
    ]
    buffers, sems = [], []
    for send, recv, kind, count in pairs:
        buffers += [pltpu.VMEM(send, kind), pltpu.VMEM(recv, kind)]
        sems += [pltpu.SemaphoreType.DMA(count), pltpu.SemaphoreType.DMA(count)]
    band = (BAND + 1) * LEN
    work = [
        pltpu.VMEM((4 * WIDTH, LEN), F32),
        pltpu.VMEM((4 * WIDTH, LEN), F32),
        pltpu.VMEM((WIDTH, LEN), F32),
        pltpu.VMEM((group, HEAD), BF16),
        pltpu.VMEM((group, HEAD), BF16),
        pltpu.VMEM((seqs, band, LEN), BF16),
        pltpu.VMEM((seqs, band, LEN), F32),
        pltpu.VMEM((seqs, HEAD, LEN), F32),
        pltpu.VMEM((seqs, 2, HEAD, LEN), F32),
        pltpu.VMEM((4 * WIDTH, LEN), BF16),
        pltpu.VMEM((64 * tabs, group), BF16),
        pltpu.VMEM((2 * seqs * tabs, LEN), BF16),
    ]

    def local(history_rows, out_grad, seg_lengths, hot_flag, hot_slot, cold_owner, cold_row, input_weight, w_out):
        vmem = pl.BlockSpec(memory_space=pltpu.VMEM)
        smem = pl.BlockSpec(memory_space=pltpu.SMEM)
        return pl.pallas_call(
            functools.partial(kernel, seqs, tabs),
            out_shape=(
                jax.ShapeDtypeStruct((512, WIDTH), F32),
                jax.ShapeDtypeStruct((64, WIDTH), F32),
            ),
            in_specs=[vmem, vmem, smem] + [vmem] * 6,
            out_specs=(vmem, vmem),
            scratch_shapes=buffers + work + sems,
            compiler_params=pltpu.CompilerParams(
                collective_id=0, has_side_effects=True, vmem_limit_bytes=48 * 1024 * 1024
            ),
        )(
            history_rows.reshape(LEN, WIDTH),
            out_grad.reshape(LEN, WIDTH),
            seg_lengths,
            hot_flag,
            hot_slot,
            cold_owner.reshape(1, LEN),
            cold_row,
            input_weight,
            w_out,
        )

    in_specs = (
        P("tab", "seq", None),
        P("tab", "seq", None),
        P("tab", None),
        P("tab", "seq"),
        P("tab", "seq"),
        P("tab", "seq", None),
        P("tab", "seq"),
        P(),
        P(),
    )
    out_specs = (P(("seq", "tab"), None), P("tab", None))
    return jax.shard_map(local, mesh=mesh, in_specs=in_specs, out_specs=out_specs, check_vma=False)
```

```python
import functools

import jax
import jax.numpy as jnp
from jax import lax
from jax.experimental import pallas as pl
from jax.experimental.pallas import tpu as pltpu
from jax.sharding import PartitionSpec as P

HEADS = 8
HEAD = 64
LEN = 128
WIDTH = 512
BAND = 4
EPS = 1e-05
MESH = pl.DeviceIdType.MESH
F32 = jnp.float32
BF16 = jnp.bfloat16
I32 = jnp.int32
VALUE, QUERY, KEY = 0, 1, 2
GATE, GATED = 0, 1
ROUND = 4
NEAR = None


def mm(a, b):
    return jnp.dot(a, b, preferred_element_type=F32)


def mm_t(a, b):
    return lax.dot_general(a, b, (((1,), (1,)), ((), ())), preferred_element_type=F32)


def sigmoid(v):
    return 0.5 * jnp.tanh(0.5 * v) + 0.5


def iota(shape, dim):
    return lax.broadcasted_iota(I32, shape, dim)


def kernel(
    seqs, tabs,
    x_hbm, og_hbm, seg_hbm, flag_hbm, slot_hbm, owner_hbm, row_hbm, w_hbm, wo_hbm,
    cold_ref, hot_ref,
    x_ref, og_ref, seg_ref, flag_ref, slot_ref, owner_ref, row_ref, w_ref, wo_ref, in_sem,
    qkv_send, qkv_recv, gg_send, gg_recv, id_send, id_recv, stat_send, stat_recv, ggr_send, ggr_recv, dg_send, dg_recv,
    row_send, row_recv, near_recv, tab_send, tab_recv, far_send, far_recv, num_send, num_recv,
    hoty_send, hoty_recv, hotz_send, hotz_recv, sum_send, sum_recv,
    proj, slope_in, xhat, keys, values, weight, slope, att, dkv, gproj, hits, own_hits, packed, table,
    send_sem, recv_sem, qkv_rs, cold_ss, cold_rs, tab_ss, tab_rs, far_ss, far_rs,
):
    me = lax.axis_index("seq")
    tab = lax.axis_index("tab")
    deep = tabs // ROUND
    z, y = tab // ROUND, lax.rem(tab, ROUND)
    chunks = deep // 2
    last = chunks - 1
    near = NEAR if NEAR is not None else chunks // 2
    lanes = 2 * ROUND
    share = 64

    def far_z(chunk, side):
        if isinstance(chunk, int):
            return deep // 2 * (1 - side) if chunk == last else (chunk + 1) * (1 - 2 * side)
        return jnp.where(chunk == last, deep // 2 * (1 - side), (chunk + 1) * (1 - 2 * side))

    def tab_peer(chunk, lane):
        return lax.rem(z + far_z(chunk, lane // ROUND) + deep, deep) * ROUND + lax.rem(lane, ROUND)

    def tab_slot(chunk, lane):
        side = lane // ROUND
        return chunk * lanes + (side if chunk == last else 1 - side) * ROUND + y

    def remote(src, dst, ss, rs, peer):
        return pltpu.make_async_remote_copy(
            src_ref=src, dst_ref=dst, send_sem=ss, recv_sem=rs, device_id=peer, device_id_type=MESH
        )

    begun = []

    class Exchange:
        def __init__(self, ss, rs, sizing):
            self.ss, self.rs, self.sizing = ss, rs, sizing
            self.left = {"sent", "got"}

        def start(self, src, dst, axis, peer):
            if self not in begun:
                begun.append(self)
            remote(src, dst, self.ss, self.rs, {axis: peer}).start()

        def sent(self):
            self.left.discard("sent")
            remote(self.sizing, self.sizing, self.ss, self.rs, {"seq": me}).wait_send()

        def got(self):
            self.left.discard("got")
            remote(self.sizing, self.sizing, self.ss, self.rs, {"seq": me}).wait_recv()

    def finish():
        for one in begun:
            for name in sorted(one.left):
                getattr(one, name)()

    def seq_all(exchange, out, into):
        for step in range(1, seqs):
            peer = lax.rem(me + step, seqs)
            exchange.start(out(peer), into, "seq", peer)

    def tab_chunk(exchange, chunk, out, into):
        def one(lane):
            exchange.start(out(lane), into.at[tab_slot(chunk, lane)], "tab", tab_peer(chunk, lane))

        if chunk == last:
            pl.loop(0, ROUND)(one)

            @pl.loop(1, ROUND)
            def _(step):
                one(ROUND + lax.rem(y + step, ROUND))
        else:
            pl.loop(0, lanes)(one)

    home = last * lanes + ROUND + y

    def tab_sizing(into, chunk):
        return into.at[pl.ds(chunk * lanes, lanes - 1 if chunk == last else lanes)]

    others = pl.ds(0, seqs - 1)
    gg = Exchange(send_sem.at[1], recv_sem.at[1], gg_recv.at[others])
    ids = Exchange(send_sem.at[2], recv_sem.at[2], id_recv.at[others])
    stat = Exchange(send_sem.at[3], recv_sem.at[3], stat_recv.at[others])
    ggr = Exchange(send_sem.at[4], recv_sem.at[4], ggr_recv.at[others])
    dg = Exchange(send_sem.at[5], recv_sem.at[5], dg_recv.at[others])
    row = Exchange(send_sem.at[6], recv_sem.at[6], row_recv.at[others])
    num = Exchange(send_sem.at[7], recv_sem.at[7], num_recv.at[pl.ds(0, tabs - 1)])
    hoty = Exchange(send_sem.at[8], recv_sem.at[8], hoty_recv.at[pl.ds(0, ROUND - 1)])
    hotz = Exchange(send_sem.at[9], recv_sem.at[9], hotz_recv.at[pl.ds(0, deep - 1)])
    total = Exchange(send_sem.at[10], recv_sem.at[10], sum_recv.at[others])
    cold = [Exchange(cold_ss.at[c], cold_rs.at[c], near_recv.at[c, others]) for c in range(near)]
    along = [Exchange(tab_ss.at[c], tab_rs.at[c], tab_sizing(tab_recv, c)) for c in range(chunks)]
    back = [Exchange(far_ss.at[c], far_rs.at[c], far_recv.at[c, others]) for c in range(chunks - near)]

    loads = [
        pltpu.make_async_copy(src, dst, in_sem.at[index])
        for index, (src, dst) in enumerate(
            (
                (flag_hbm, flag_ref),
                (slot_hbm, slot_ref),
                (owner_hbm, owner_ref),
                (row_hbm, row_ref),
                (x_hbm, x_ref),
                (w_hbm.at[:, pl.ds(WIDTH, 3 * WIDTH)], w_ref.at[:, pl.ds(WIDTH, 3 * WIDTH)]),
                (seg_hbm, seg_ref),
                (og_hbm, og_ref),
                (wo_hbm, wo_ref),
                (w_hbm.at[:, pl.ds(0, WIDTH)], w_ref.at[:, pl.ds(0, WIDTH)]),
            )
        )
    ]
    for load in loads:
        load.start()

    barrier = pltpu.get_barrier_semaphore()
    for step in range(1, seqs):
        pl.semaphore_signal(barrier, inc=1, device_id={"seq": lax.rem(me + step, seqs)}, device_id_type=MESH)

    @pl.loop(1, tabs)
    def _(step):
        pl.semaphore_signal(barrier, inc=1, device_id={"tab": lax.rem(tab + step, tabs)}, device_id_type=MESH)

    for load in loads[:4]:
        load.wait()
    flag = flag_ref[...]
    owner = jnp.where(flag == 1, -1, owner_ref[...])
    owner_row = jnp.broadcast_to(owner.astype(F32), (LEN, LEN))
    earlier = (owner_row.T == owner_row) & (iota((LEN, LEN), 0) < iota((LEN, LEN), 1))
    taken = jnp.sum(jnp.where(earlier, 1.0, 0.0), axis=0, keepdims=True)
    lane_of = jnp.where(flag == 1, -1, owner * 2 + taken.astype(I32))
    which = iota((8, LEN), 0)
    id_send[...] = jnp.where(
        which == 0,
        jnp.where(flag == 1, slot_ref[...], -1),
        jnp.where(which == 1, lane_of, jnp.where(which == 2, row_ref[...], 0)),
    )
    id_recv[me] = id_send[...]

    loads[4].wait()
    wide = x_ref[...].astype(F32)
    centered = wide - jnp.mean(wide, axis=1, keepdims=True)
    normed = centered * lax.rsqrt(jnp.mean(centered * centered, axis=1, keepdims=True) + EPS)
    xin = normed.astype(BF16)
    pl.semaphore_wait(barrier, seqs - 1 + tabs - 1)
    seq_all(ids, lambda peer: id_send, id_recv.at[me])

    def project(block, pair):
        spot = pl.multiple_of(block * WIDTH + pair * LEN, LEN)
        out = mm(xin, w_ref[:, pl.ds(spot, LEN)]).T
        proj[pl.ds(spot, LEN), :] = out
        return (out * sigmoid(out)).astype(BF16).reshape(2, HEAD, LEN)

    def qkv_copy(peer):
        return remote(qkv_send.at[peer], qkv_recv.at[me], send_sem.at[0], qkv_rs.at[me], {"seq": peer})

    loads[5].wait()
    for step in range(HEADS // 2):
        pair = lax.rem(me // 2 + 1 + step, HEADS // 2)
        for part, block in ((VALUE, 1), (QUERY, 2), (KEY, 3)):
            qkv_send[pl.ds(2 * pair, 2), part] = project(block, pair)
        for core in range(2):
            peer = 2 * pair + core

            @pl.when(peer != me)
            def _():
                qkv_copy(peer).start()

    qkv_recv[me] = qkv_send[me]

    for load in loads[6:]:
        load.wait()
    for step in range(HEADS // 2):
        pair = lax.rem(me // 2 + 1 + step, HEADS // 2)
        spot = pl.multiple_of(pair * LEN, LEN)
        gg_send[pl.ds(2 * pair, 2), GATE] = project(0, pair)
        gg_send[pl.ds(2 * pair, 2), GATED] = mm_t(wo_ref[pl.ds(spot, LEN), :], og_ref[...]).astype(BF16).reshape(2, HEAD, LEN)
        for core in range(2):
            peer = 2 * pair + core

            @pl.when(peer != me)
            def _():
                gg.start(gg_send.at[peer], gg_recv.at[me], "seq", peer)

    gg_recv[me] = gg_send[me]

    ids.got()
    for chunk in range(chunks):
        place = iota((lanes * 2 * seqs, LEN), 0)
        lane, source_of = place >> 4, (place >> 1) & (seqs - 1)
        wanted = (me * tabs + tab_peer(chunk, lane)) * 2 + (place & 1)
        numbers = jnp.zeros((lanes * 2 * seqs, LEN), F32)
        for source in range(seqs):
            pick = jnp.where(jnp.where(source_of == source, wanted, -5) == id_recv[source, 1:2, :], 1.0, 0.0).astype(BF16)
            number = id_recv[source, 2:3, :]
            line = iota((LEN, LEN), 0)
            halves = jnp.where(line == 0, number >> 4, jnp.where(line == 1, number & 15, 0))
            numbers = numbers + mm_t(pick, halves.astype(F32).astype(BF16))
        num_send[pl.ds(chunk * lanes, lanes)] = numbers.astype(BF16).reshape(lanes, 2 * seqs, LEN)
        tab_chunk(num, chunk, lambda lane: num_send.at[chunk * lanes + lane], num_recv)
    num_recv[home] = num_send[home]

    for chunk in range(chunks):
        place = iota((lanes * 2 * seqs, LEN), 0)
        major, minor = place >> 4, (place >> 1) & 7
        to_seq, lane = (major, minor) if chunk < near else (minor, major)
        wanted = (to_seq * tabs + tab_peer(chunk, lane)) * 2 + (place & 1)
        own_hits[chunk] = jnp.where(wanted == id_send[1:2, :], 1.0, 0.0).astype(BF16)

    end0 = seg_ref[0, 0]
    end1 = end0 + seg_ref[0, 1]
    end2 = end1 + seg_ref[0, 2]
    for block in range(seqs):
        low = max(0, block - BAND)
        count = block + 1 - low

        @pl.when(block != me)
        def _():
            slab = qkv_recv.at[block]
            remote(slab, slab, send_sem.at[0], qkv_rs.at[block], {"seq": me}).wait_recv()

        keys[pl.ds(block * LEN, LEN), :] = qkv_recv[block, KEY].astype(F32).T.astype(BF16)
        values[pl.ds(block * LEN, LEN), :] = qkv_recv[block, VALUE].astype(F32).T.astype(BF16)
        score = mm(keys[pl.ds(low * LEN, count * LEN), :], qkv_recv[block, QUERY]) * 0.125
        here = block * LEN + iota((1, LEN), 1)
        start = jnp.where(here >= end2, end2, jnp.where(here >= end1, end1, jnp.where(here >= end0, end0, 0)))
        there = low * LEN + iota(score.shape, 0)
        allowed = (there >= start) & (there <= here)
        gate = sigmoid(score)
        swish = score * gate
        heavy = jnp.where(allowed, swish, 0.0).astype(BF16)
        weight[block, pl.ds(0, count * LEN), :] = heavy
        slope[block, pl.ds(0, count * LEN), :] = jnp.where(allowed, (gate + swish * (1.0 - gate)) * 0.125, 0.0)
        across = jnp.concatenate([qkv_recv[other, VALUE] for other in range(low, block + 1)], axis=1)
        att[block] = mm(across, heavy)
    gg.got()
    for block in range(seqs):
        mixed = att[block]
        grad = gg_recv[block, GATE].astype(F32) * gg_recv[block, GATED].astype(F32)
        mean = jnp.mean(mixed, axis=0, keepdims=True)
        off = mixed - mean
        stat_send[0, pl.ds(block, 1), :] = mean
        stat_send[1, pl.ds(block, 1), :] = jnp.sum(off * off, axis=0, keepdims=True)
        stat_send[2, pl.ds(block, 1), :] = jnp.sum(grad, axis=0, keepdims=True)
        stat_send[3, pl.ds(block, 1), :] = jnp.sum(grad * off, axis=0, keepdims=True)
    seq_all(stat, lambda peer: stat_send, stat_recv.at[me])
    stat_recv[me] = stat_send[...]

    across = x_ref[...].astype(F32).T
    across = across - jnp.mean(across, axis=0, keepdims=True)
    inv_in = lax.rsqrt(jnp.mean(across * across, axis=0, keepdims=True) + EPS)
    xhat[...] = across * inv_in

    @pl.loop(0, 4)
    def _(block):
        span = pl.ds(pl.multiple_of(block * WIDTH, WIDTH), WIDTH)
        value = proj[span, :]
        gate = sigmoid(value)
        slope_in[span, :] = gate * (1.0 + value * (1.0 - gate))

    hot_ids = jnp.concatenate([id_recv[source, 0:1, :] for source in range(seqs)], axis=1)

    def hot_table(block):
        spot = pl.multiple_of(block * LEN, LEN)
        hits[pl.ds(spot, LEN), :] = jnp.where(iota((LEN, seqs * LEN), 0) + spot == hot_ids, 1.0, 0.0).astype(BF16)

    tables = hits.shape[0] // LEN
    pl.loop(0, tables // 2)(hot_table)
    ids.sent()
    gg.sent()
    remote(qkv_recv.at[others], qkv_recv.at[others], send_sem.at[0], qkv_rs.at[0], {"seq": me}).wait_send()

    stat.got()
    means = [stat_recv[source, 0] for source in range(seqs)]
    mean = sum(means) * (1.0 / seqs)
    spread = sum(stat_recv[source, 1] + HEAD * (means[source] - mean) ** 2 for source in range(seqs))
    inv = lax.rsqrt(spread * (1.0 / WIDTH) + EPS)
    first = sum(stat_recv[source, 2] for source in range(seqs)) * (1.0 / WIDTH)
    second = sum(stat_recv[source, 3] + (means[source] - mean) * stat_recv[source, 2] for source in range(seqs))
    second = inv * second * (1.0 / WIDTH)

    for block in range(seqs):
        def line(array):
            return array[block : block + 1, :]

        gated = gg_recv[block, GATED].astype(F32)
        normed_here = (att[block] - line(mean)) * line(inv)
        ggr_send[block] = (gated * normed_here).astype(BF16)
        att[block] = line(inv) * (gg_recv[block, GATE].astype(F32) * gated - line(first) - normed_here * line(second))
    seq_all(ggr, lambda peer: ggr_send.at[peer], ggr_recv.at[me])
    ggr_recv[me] = ggr_send[me]

    for block in reversed(range(seqs)):
        low = max(0, block - BAND)
        count = block + 1 - low
        grad = att[block].astype(BF16)
        query = qkv_recv[block, QUERY]
        span = pl.ds(low * LEN, count * LEN)
        grad_weight = mm(values[span, :], grad)
        grad_score = (grad_weight * slope[block, pl.ds(0, count * LEN), :]).astype(BF16)
        across = jnp.concatenate([qkv_recv[other, KEY] for other in range(low, block + 1)], axis=1)
        grad_value = mm_t(grad, weight[block, pl.ds(0, count * LEN), :])
        grad_key = mm_t(query, grad_score)
        dg_send[block, QUERY] = mm(across, grad_score).astype(BF16)
        for other in range(low, block + 1):
            cut = slice((other - low) * LEN, (other - low + 1) * LEN)
            new_value, new_key = grad_value[:, cut], grad_key[:, cut]
            if block < min(seqs - 1, other + BAND):
                new_value, new_key = new_value + dkv[other, 0], new_key + dkv[other, 1]
            if other == block:
                dg_send[block, VALUE] = new_value.astype(BF16)
                dg_send[block, KEY] = new_key.astype(BF16)
            else:
                dkv[other, 0] = new_value
                dkv[other, 1] = new_key

        @pl.when(block != me)
        def _():
            dg.start(dg_send.at[block], dg_recv.at[me], "seq", block)

    dg_recv[me] = dg_send[me]

    pl.loop(tables // 2, tables)(hot_table)
    out_at, in_at = iota((LEN, LEN), 0), iota((LEN, LEN), 1)
    order = jnp.where(
        ((out_at >> 4) == ((in_at >> 1) & 7)) & (((out_at >> 1) & 7) == (in_at >> 4)) & ((out_at & 1) == (in_at & 1)), 1.0, 0.0
    ).astype(BF16)
    num.got()
    line, column = iota((8, LEN), 0), iota((8, LEN), 1)
    scale = jnp.where(line == 0, jnp.where(column == 0, 16.0, jnp.where(column == 1, 1.0, 0.0)), 0.0).astype(BF16)
    for chunk in range(chunks):
        numbers = num_recv[pl.ds(chunk * lanes, lanes)].reshape(LEN, LEN)
        if chunk >= near:
            numbers = mm(order, numbers).astype(BF16)
        numbers = mm_t(scale, numbers)[0:1, :].astype(I32)
        table[:, pl.ds(chunk * LEN, LEN)] = jnp.where(iota((cold_ref.shape[0], LEN), 0) == numbers, 1.0, 0.0).astype(BF16)
    num.sent()
    stat.sent()
    ggr.got()
    gproj[0:WIDTH, :] = (ggr_recv[...].reshape(WIDTH, LEN).astype(F32) * slope_in[0:WIDTH, :]).astype(BF16)
    grad_in = mm(w_ref[:, 0:WIDTH], gproj[0:WIDTH, :])
    ggr.sent()
    dg.got()
    for part in range(3):
        span = pl.ds((part + 1) * WIDTH, WIDTH)
        gproj[span, :] = (dg_recv[:, part].reshape(WIDTH, LEN).astype(F32) * slope_in[span, :]).astype(BF16)
    grad_in = grad_in + mm(w_ref[:, WIDTH:], gproj[WIDTH:, :])
    norm_in = xhat[...]
    grad_rows = og_ref[...].astype(F32).T + inv_in * (
        grad_in
        - jnp.mean(grad_in, axis=0, keepdims=True)
        - norm_in * jnp.mean(grad_in * norm_in, axis=0, keepdims=True)
    )
    grad_rows = grad_rows.astype(BF16)

    row_send[...] = grad_rows.reshape(row_send.shape)
    seq_all(row, lambda peer: row_send.at[peer], row_recv.at[me])
    row_recv[me] = row_send[me]

    for chunk in reversed(range(chunks)):
        packed[chunk] = mm_t(own_hits[chunk], grad_rows).astype(BF16).reshape(seqs, 2 * seqs, WIDTH)
        if chunk < near:
            seq_all(cold[chunk], lambda peer: packed.at[chunk, peer], near_recv.at[chunk, me])
            near_recv[chunk, me] = packed[chunk, me]
        else:
            tab_chunk(along[chunk], chunk, lambda lane: packed.at[chunk, lane], tab_recv)
            if chunk == last:
                tab_recv[home] = packed[chunk, ROUND + y]
    dg.sent()

    row.got()
    slab = jnp.concatenate([row_recv[source] for source in range(seqs)], axis=1)
    left = iota((HEAD // 2, LEN), 1) < share
    for chunk in range(chunks):
        sums = mm_t(slab, hits[pl.ds(chunk * lanes * share, lanes * share), :])
        for two in range(lanes // 2):
            both = sums[:, two * LEN : (two + 1) * LEN]
            upper, lower = both[: HEAD // 2], both[HEAD // 2 :]
            plane, owner_y = 2 * chunk + 2 * two // ROUND, 2 * two % ROUND
            hoty_send[owner_y, plane] = jnp.where(left, upper, pltpu.roll(lower, share, 1)).astype(BF16)
            hoty_send[owner_y + 1, plane] = jnp.where(left, pltpu.roll(upper, share, 1), lower).astype(BF16)
    for step in range(1, ROUND):
        peer = lax.rem(y + step, ROUND)
        hoty.start(hoty_send.at[peer], hoty_recv.at[y], "tab", z * ROUND + peer)
    hoty_recv[y] = hoty_send[y]

    for chunk in reversed(range(near)):
        cold[chunk].got()
        rows = mm(order, near_recv[chunk].reshape(LEN, WIDTH)).astype(BF16)
        tab_send[chunk] = rows.reshape(lanes, 2 * seqs, WIDTH)
        tab_chunk(along[chunk], chunk, lambda lane: tab_send.at[chunk, lane], tab_recv)
        if chunk == last:
            tab_recv[home] = tab_send[chunk, ROUND + y]

    hoty.got()
    for plane in range(deep):
        sums = sum(hoty_recv[source, plane].astype(F32) for source in range(ROUND))
        hotz_send[plane] = sums.astype(BF16)
    for step in range(1, deep):
        peer = lax.rem(z + step, deep)
        hotz.start(hotz_send.at[peer], hotz_recv.at[z], "tab", peer * ROUND + y)
    hotz_recv[z] = hotz_send[z]

    for chunk in reversed(range(near, chunks)):
        along[chunk].got()
        rows = mm(order, tab_recv[pl.ds(chunk * lanes, lanes)].reshape(LEN, WIDTH)).astype(BF16)
        far_send[chunk - near] = rows.reshape(seqs, 2 * lanes, WIDTH)
        seq_all(back[chunk - near], lambda peer: far_send.at[chunk - near, peer], far_recv.at[chunk - near, me])
        far_recv[chunk - near, me] = far_send[chunk - near, me]

    hotz.got()
    sum_send[...] = sum(hotz_recv[source].astype(F32) for source in range(deep))
    seq_all(total, lambda peer: sum_send, sum_recv.at[me])
    sum_recv[me] = sum_send[...]
    row.sent()
    hoty.sent()
    hotz.sent()
    for part in cold:
        part.sent()
    for chunk in range(near, chunks):
        along[chunk].sent()

    for chunk in range(near):
        along[chunk].got()
    result = jnp.zeros(cold_ref.shape, F32)
    if near:
        result = mm(table[:, : near * LEN], tab_recv[0 : near * lanes].reshape(near * LEN, WIDTH))
    for part in back:
        part.got()
    if near < chunks:
        result = result + mm(table[:, near * LEN :], far_recv[...].reshape((chunks - near) * LEN, WIDTH))
    cold_ref[...] = result

    total.got()
    stacked = []
    for source in range(seqs):
        piece = sum_recv[source]
        stacked += [piece, pltpu.roll(piece, share, 1)]
    hot_ref[...] = jnp.concatenate(stacked, axis=0).T[:share, :]

    finish()


def solution(mesh):
    seqs, tabs = mesh.shape["seq"], mesh.shape["tab"]
    deep = tabs // ROUND
    chunks = deep // 2
    near = NEAR if NEAR is not None else chunks // 2
    lanes = 2 * ROUND
    group = seqs * LEN
    inputs = [
        pltpu.VMEM((LEN, WIDTH), BF16),
        pltpu.VMEM((LEN, WIDTH), BF16),
        pltpu.SMEM((1, 4), I32),
        pltpu.VMEM((1, LEN), I32),
        pltpu.VMEM((1, LEN), I32),
        pltpu.VMEM((1, LEN), I32),
        pltpu.VMEM((1, LEN), I32),
        pltpu.VMEM((WIDTH, 4 * WIDTH), BF16),
        pltpu.VMEM((WIDTH, WIDTH), BF16),
        pltpu.SemaphoreType.DMA((10,)),
    ]
    exchanged = [
        pltpu.VMEM((HEADS, 3, HEAD, LEN), BF16),
        pltpu.VMEM((seqs, 3, HEAD, LEN), BF16),
        pltpu.VMEM((HEADS, 2, HEAD, LEN), BF16),
        pltpu.VMEM((seqs, 2, HEAD, LEN), BF16),
        pltpu.VMEM((8, LEN), I32),
        pltpu.VMEM((seqs, 8, LEN), I32),
        pltpu.VMEM((4, 8, LEN), F32),
        pltpu.VMEM((seqs, 4, 8, LEN), F32),
        pltpu.VMEM((seqs, HEAD, LEN), BF16),
        pltpu.VMEM((HEADS, HEAD, LEN), BF16),
        pltpu.VMEM((seqs, 3, HEAD, LEN), BF16),
        pltpu.VMEM((HEADS, 3, HEAD, LEN), BF16),
        pltpu.VMEM((seqs, HEAD, LEN), BF16),
        pltpu.VMEM((seqs, HEAD, LEN), BF16),
        pltpu.VMEM((max(near, 1), seqs, 2 * lanes, WIDTH), BF16),
        pltpu.VMEM((max(near, 1), lanes, 2 * seqs, WIDTH), BF16),
        pltpu.VMEM((tabs, 2 * seqs, WIDTH), BF16),
        pltpu.VMEM((max(chunks - near, 1), seqs, 2 * lanes, WIDTH), BF16),
        pltpu.VMEM((max(chunks - near, 1), seqs, 2 * lanes, WIDTH), BF16),
        pltpu.VMEM((tabs, 2 * seqs, LEN), BF16),
        pltpu.VMEM((tabs, 2 * seqs, LEN), BF16),
        pltpu.VMEM((ROUND, deep, HEAD // 2, LEN), BF16),
        pltpu.VMEM((ROUND, deep, HEAD // 2, LEN), BF16),
        pltpu.VMEM((deep, HEAD // 2, LEN), BF16),
        pltpu.VMEM((deep, HEAD // 2, LEN), BF16),
        pltpu.VMEM((HEAD // 2, LEN), F32),
        pltpu.VMEM((seqs, HEAD // 2, LEN), F32),
    ]
    band = (BAND + 1) * LEN
    work = [
        pltpu.VMEM((4 * WIDTH, LEN), F32),
        pltpu.VMEM((4 * WIDTH, LEN), F32),
        pltpu.VMEM((WIDTH, LEN), F32),
        pltpu.VMEM((group, HEAD), BF16),
        pltpu.VMEM((group, HEAD), BF16),
        pltpu.VMEM((seqs, band, LEN), BF16),
        pltpu.VMEM((seqs, band, LEN), F32),
        pltpu.VMEM((seqs, HEAD, LEN), F32),
        pltpu.VMEM((seqs, 2, HEAD, LEN), F32),
        pltpu.VMEM((4 * WIDTH, LEN), BF16),
        pltpu.VMEM((64 * tabs, group), BF16),
        pltpu.VMEM((chunks, LEN, LEN), BF16),
        pltpu.VMEM((chunks, seqs, 2 * seqs, WIDTH), BF16),
        pltpu.VMEM((512, chunks * LEN), BF16),
    ]
    dma = pltpu.SemaphoreType.DMA
    sems = [dma((11,)), dma((11,)), dma((seqs,))] + [dma((chunks,)) for _ in range(6)]

    def local(history_rows, out_grad, seg_lengths, hot_flag, hot_slot, cold_owner, cold_row, input_weight, w_out):
        vmem = pl.BlockSpec(memory_space=pltpu.VMEM)
        return pl.pallas_call(
            functools.partial(kernel, seqs, tabs),
            out_shape=(
                jax.ShapeDtypeStruct((512, WIDTH), F32),
                jax.ShapeDtypeStruct((64, WIDTH), F32),
            ),
            in_specs=[pl.BlockSpec(memory_space=pltpu.HBM)] * 9,
            out_specs=(vmem, vmem),
            scratch_shapes=inputs + exchanged + work + sems,
            compiler_params=pltpu.CompilerParams(
                collective_id=0, has_side_effects=True, vmem_limit_bytes=56 * 1024 * 1024
            ),
        )(
            history_rows.reshape(LEN, WIDTH),
            out_grad.reshape(LEN, WIDTH),
            seg_lengths,
            hot_flag,
            hot_slot,
            cold_owner.reshape(1, LEN),
            cold_row,
            input_weight,
            w_out,
        )

    in_specs = (
        P("tab", "seq", None),
        P("tab", "seq", None),
        P("tab", None),
        P("tab", "seq"),
        P("tab", "seq"),
        P("tab", "seq", None),
        P("tab", "seq"),
        P(),
        P(),
    )
    out_specs = (P(("seq", "tab"), None), P("tab", None))
    return jax.shard_map(local, mesh=mesh, in_specs=in_specs, out_specs=out_specs, check_vma=False)
```

```python
import functools

import jax
import jax.numpy as jnp
from jax import lax
from jax.experimental import pallas as pl
from jax.experimental.pallas import tpu as pltpu
from jax.sharding import PartitionSpec as P

HEADS = 8
HEAD = 64
LEN = 128
WIDTH = 512
BAND = 4
EPS = 1e-05
MESH = pl.DeviceIdType.MESH
F32 = jnp.float32
BF16 = jnp.bfloat16
I32 = jnp.int32
VALUE, QUERY, KEY = 0, 1, 2
ROUND = 4
NEAR = None


def mm(a, b):
    return jnp.dot(a, b, preferred_element_type=F32)


def mm_t(a, b):
    return lax.dot_general(a, b, (((1,), (1,)), ((), ())), preferred_element_type=F32)


def sigmoid(v):
    return 0.5 * jnp.tanh(0.5 * v) + 0.5


def iota(shape, dim):
    return lax.broadcasted_iota(I32, shape, dim)


def kernel(
    seqs, tabs,
    x_hbm, og_hbm, seg_hbm, flag_hbm, slot_hbm, owner_hbm, row_hbm, w_hbm, wo_hbm,
    cold_ref, hot_ref,
    x_ref, og_ref, seg_ref, flag_ref, slot_ref, owner_ref, row_ref, w_ref, wo_ref, in_sem,
    qkv_send, qkv_recv, n_send, n_recv, id_send, id_recv, stat_send, stat_recv, off_send, off_recv, dg_send, dg_recv,
    row_send, row_recv, near_send, near_recv, tab_send, tab_recv, far_send, far_recv, numy_send, numy_recv, numz_recv,
    hoty_send, hoty_recv, hotz_send, hotz_recv, sum_send, sum_recv,
    proj, slope_in, xhat, gated, keys, values, weight, slope, att, dkv, gproj, hits, own_hits, packed, table,
    send_sem, recv_sem, qkv_rs, cold_ss, cold_rs, tab_ss, tab_rs, far_ss, far_rs,
):
    me = lax.axis_index("seq")
    tab = lax.axis_index("tab")
    deep = tabs // ROUND
    z, y = tab // ROUND, lax.rem(tab, ROUND)
    chunks = deep // 2
    last = chunks - 1
    near = NEAR if NEAR is not None else chunks // 2
    lanes = 2 * ROUND
    share = 64

    def far_z(chunk, side):
        if isinstance(chunk, int):
            return deep // 2 * (1 - side) if chunk == last else (chunk + 1) * (1 - 2 * side)
        return jnp.where(chunk == last, deep // 2 * (1 - side), (chunk + 1) * (1 - 2 * side))

    def tab_peer(chunk, lane):
        return lax.rem(z + far_z(chunk, lane // ROUND) + deep, deep) * ROUND + lax.rem(lane, ROUND)

    def tab_slot(chunk, lane):
        side = lane // ROUND
        return chunk * lanes + (side if chunk == last else 1 - side) * ROUND + y

    def remote(src, dst, ss, rs, peer):
        return pltpu.make_async_remote_copy(
            src_ref=src, dst_ref=dst, send_sem=ss, recv_sem=rs, device_id=peer, device_id_type=MESH
        )

    begun = []

    class Exchange:
        def __init__(self, ss, rs, sizing):
            self.ss, self.rs, self.sizing = ss, rs, sizing
            self.left = {"sent", "got"}

        def start(self, src, dst, axis, peer):
            if self not in begun:
                begun.append(self)
            remote(src, dst, self.ss, self.rs, {axis: peer}).start()

        def sent(self):
            self.left.discard("sent")
            remote(self.sizing, self.sizing, self.ss, self.rs, {"seq": me}).wait_send()

        def got(self):
            self.left.discard("got")
            remote(self.sizing, self.sizing, self.ss, self.rs, {"seq": me}).wait_recv()

    def finish():
        for one in begun:
            for name in sorted(one.left):
                getattr(one, name)()

    def seq_all(exchange, out, into):
        for step in range(1, seqs):
            peer = lax.rem(me + step, seqs)
            exchange.start(out(peer), into, "seq", peer)

    def tab_chunk(exchange, chunk, out, into):
        def one(lane):
            exchange.start(out(lane), into.at[tab_slot(chunk, lane)], "tab", tab_peer(chunk, lane))

        if chunk == last:
            pl.loop(0, ROUND)(one)

            @pl.loop(1, ROUND)
            def _(step):
                one(ROUND + lax.rem(y + step, ROUND))
        else:
            pl.loop(0, lanes)(one)

    home = last * lanes + ROUND + y

    def tab_sizing(into, chunk):
        return into.at[pl.ds(chunk * lanes, lanes - 1 if chunk == last else lanes)]

    others = pl.ds(0, seqs - 1)
    ns = Exchange(send_sem.at[1], recv_sem.at[1], n_recv.at[others])
    ids = Exchange(send_sem.at[2], recv_sem.at[2], id_recv.at[others])
    stats = [Exchange(send_sem.at[3 + half], recv_sem.at[3 + half], stat_recv.at[half, others]) for half in range(2)]
    offs = Exchange(send_sem.at[5], recv_sem.at[5], off_recv.at[others])
    dg = Exchange(send_sem.at[6], recv_sem.at[6], dg_recv.at[others])
    row = Exchange(send_sem.at[7], recv_sem.at[7], row_recv.at[others])
    numy = Exchange(send_sem.at[8], recv_sem.at[8], numy_recv.at[pl.ds(0, ROUND - 1)])
    numz = Exchange(send_sem.at[9], recv_sem.at[9], numz_recv.at[pl.ds(0, deep - 1)])
    hoty = Exchange(send_sem.at[10], recv_sem.at[10], hoty_recv.at[pl.ds(0, ROUND - 1)])
    hotz = Exchange(send_sem.at[11], recv_sem.at[11], hotz_recv.at[pl.ds(0, deep - 1)])
    total = Exchange(send_sem.at[12], recv_sem.at[12], sum_recv.at[others])
    cold = Exchange(cold_ss.at[0], cold_rs.at[0], near_recv.at[others])
    along = [Exchange(tab_ss.at[c], tab_rs.at[c], tab_sizing(tab_recv, c)) for c in range(chunks)]
    back = [Exchange(far_ss.at[c], far_rs.at[c], far_recv.at[c, others]) for c in range(chunks - near)]

    loads = [
        pltpu.make_async_copy(src, dst, in_sem.at[index])
        for index, (src, dst) in enumerate(
            (
                (flag_hbm, flag_ref),
                (slot_hbm, slot_ref),
                (owner_hbm, owner_ref),
                (row_hbm, row_ref),
                (x_hbm, x_ref),
                (w_hbm.at[:, pl.ds(WIDTH, 3 * WIDTH)], w_ref.at[:, pl.ds(WIDTH, 3 * WIDTH)]),
                (seg_hbm, seg_ref),
                (og_hbm, og_ref),
                (wo_hbm, wo_ref),
                (w_hbm.at[:, pl.ds(0, WIDTH)], w_ref.at[:, pl.ds(0, WIDTH)]),
            )
        )
    ]
    for load in loads:
        load.start()

    barrier = pltpu.get_barrier_semaphore()
    for step in range(1, seqs):
        pl.semaphore_signal(barrier, inc=1, device_id={"seq": lax.rem(me + step, seqs)}, device_id_type=MESH)

    for step in range(1, ROUND):
        peer = z * ROUND + lax.rem(y + step, ROUND)
        pl.semaphore_signal(barrier, inc=1, device_id={"tab": peer}, device_id_type=MESH)
    for step in range(1, deep):
        peer = lax.rem(z + step, deep) * ROUND + y
        pl.semaphore_signal(barrier, inc=1, device_id={"tab": peer}, device_id_type=MESH)

    for load in loads[:4]:
        load.wait()
    flag = flag_ref[...]
    owner = jnp.where(flag == 1, -1, owner_ref[...])
    owner_row = jnp.broadcast_to(owner.astype(F32), (LEN, LEN))
    earlier = (owner_row.T == owner_row) & (iota((LEN, LEN), 0) < iota((LEN, LEN), 1))
    taken = jnp.sum(jnp.where(earlier, 1.0, 0.0), axis=0, keepdims=True)
    lane_of = jnp.where(flag == 1, -1, owner * 2 + taken.astype(I32))
    which = iota((8, LEN), 0)
    id_send[...] = jnp.where(
        which == 0,
        jnp.where(flag == 1, slot_ref[...], -1),
        jnp.where(which == 1, lane_of, jnp.where(which == 2, row_ref[...], 0)),
    )
    id_recv[me] = id_send[...]

    loads[4].wait()
    wide = x_ref[...].astype(F32)
    centered = wide - jnp.mean(wide, axis=1, keepdims=True)
    normed = centered * lax.rsqrt(jnp.mean(centered * centered, axis=1, keepdims=True) + EPS)
    xin = normed.astype(BF16)
    pl.semaphore_wait(barrier, seqs - 1 + ROUND - 1 + deep - 1)

    def project(block, pair):
        spot = pl.multiple_of(block * WIDTH + pair * LEN, LEN)
        out = mm(xin, w_ref[:, pl.ds(spot, LEN)]).T
        proj[pl.ds(spot, LEN), :] = out
        return (out * sigmoid(out)).astype(BF16).reshape(2, HEAD, LEN)

    def qkv_copy(peer):
        return remote(qkv_send.at[peer], qkv_recv.at[me], send_sem.at[0], qkv_rs.at[me], {"seq": peer})

    loads[5].wait()
    for step in range(HEADS // 2):
        pair = lax.rem(me // 2 + 1 + step, HEADS // 2)
        for part, block in ((VALUE, 1), (QUERY, 2), (KEY, 3)):
            qkv_send[pl.ds(2 * pair, 2), part] = project(block, pair)
        for core in range(2):
            peer = 2 * pair + core

            @pl.when(peer != me)
            def _():
                qkv_copy(peer).start()

    qkv_recv[me] = qkv_send[me]

    for load in loads[6:]:
        load.wait()
    for step in range(HEADS // 2):
        pair = lax.rem(me // 2 + 1 + step, HEADS // 2)
        spot = pl.multiple_of(pair * LEN, LEN)
        up = mm_t(wo_ref[pl.ds(spot, LEN), :], og_ref[...])
        gated[pl.ds(spot, LEN), :] = up
        n_send[pl.ds(2 * pair, 2)] = (up.reshape(2, HEAD, LEN) * project(0, pair).astype(F32)).astype(BF16)
        for core in range(2):
            peer = 2 * pair + core

            @pl.when(peer != me)
            def _():
                ns.start(n_send.at[peer], n_recv.at[me], "seq", peer)

    n_recv[me] = n_send[me]
    seq_all(ids, lambda peer: id_send, id_recv.at[me])

    for chunk in range(chunks):
        place = iota((lanes * 2 * seqs, LEN), 0)
        major, minor = place >> 4, (place >> 1) & 7
        to_seq, lane = (major, minor) if chunk < near else (minor, major)
        wanted = (to_seq * tabs + tab_peer(chunk, lane)) * 2 + (place & 1)
        own_hits[chunk] = jnp.where(wanted == id_send[1:2, :], 1.0, 0.0).astype(BF16)

    end0 = seg_ref[0, 0]
    end1 = end0 + seg_ref[0, 1]
    end2 = end1 + seg_ref[0, 2]
    for block in range(seqs):
        @pl.when(block != me)
        def _():
            slab = qkv_recv.at[block]
            remote(slab, slab, send_sem.at[0], qkv_rs.at[block], {"seq": me}).wait_recv()

        keys[pl.ds(block * LEN, LEN), :] = qkv_recv[block, KEY].astype(F32).T.astype(BF16)
        values[pl.ds(block * LEN, LEN), :] = qkv_recv[block, VALUE].astype(F32).T.astype(BF16)

    half = seqs // 2
    for block in reversed(range(seqs)):
        low = max(0, block - BAND)
        count = block + 1 - low
        score = mm(keys[pl.ds(low * LEN, count * LEN), :], qkv_recv[block, QUERY]) * 0.125
        here = block * LEN + iota((1, LEN), 1)
        start = jnp.where(here >= end2, end2, jnp.where(here >= end1, end1, jnp.where(here >= end0, end0, 0)))
        there = low * LEN + iota(score.shape, 0)
        allowed = (there >= start) & (there <= here)
        gate = sigmoid(score)
        swish = score * gate
        heavy = jnp.where(allowed, swish, 0.0).astype(BF16)
        weight[block, pl.ds(0, count * LEN), :] = heavy
        slope[block, pl.ds(0, count * LEN), :] = jnp.where(allowed, (gate + swish * (1.0 - gate)) * 0.125, 0.0)
        across = jnp.concatenate([qkv_recv[other, VALUE] for other in range(low, block + 1)], axis=1)
        mixed = mm(across, heavy)
        if block == seqs - 1:
            ns.got()
        grad = n_recv[block].astype(F32)
        mean = jnp.mean(mixed, axis=0, keepdims=True)
        off = mixed - mean
        att[block] = off
        off_send[block] = off.astype(BF16)
        part, line = block // half, block % half
        for kind, sums in enumerate(
            (
                mean,
                jnp.sum(off * off, axis=0, keepdims=True),
                jnp.sum(grad, axis=0, keepdims=True),
                jnp.sum(grad * off, axis=0, keepdims=True),
            )
        ):
            stat_send[part, pl.ds(kind * half + line, 1), :] = sums
        if line == 0:
            seq_all(stats[part], lambda peer: stat_send.at[part], stat_recv.at[part, me])
            stat_recv[part, me] = stat_send[part]
    seq_all(offs, lambda peer: off_send.at[peer], off_recv.at[me])
    off_recv[me] = off_send[me]

    ids.got()
    place = iota((LEN, LEN), 0)
    for step in range(ROUND):
        peer = lax.rem(y + 1 + step, ROUND)
        wanted = (me * tabs + (place >> 4) * ROUND + peer) * 2 + (place & 1)
        numbers = jnp.zeros((2 * seqs, LEN), F32)
        for source in range(seqs):
            mine = jnp.where(((place >> 1) & (seqs - 1)) == source, wanted, -5)
            pick = jnp.where(mine == id_recv[source, 1:2, :], 1.0, 0.0).astype(BF16)
            number = id_recv[source, 2:3, :]
            line = iota((2 * seqs, LEN), 0)
            halves = jnp.where(line == 0, number >> 4, jnp.where(line == 1, number & 15, 0))
            numbers = numbers + mm_t(halves.astype(F32).astype(BF16), pick)
        numy_send[peer] = numbers.astype(BF16)
        if step < ROUND - 1:
            numy.start(numy_send.at[peer], numy_recv.at[y], "tab", z * ROUND + peer)
    numy_recv[y] = numy_send[y]

    across = x_ref[...].astype(F32).T
    across = across - jnp.mean(across, axis=0, keepdims=True)
    inv_in = lax.rsqrt(jnp.mean(across * across, axis=0, keepdims=True) + EPS)
    xhat[...] = across * inv_in

    @pl.loop(0, 4)
    def _(block):
        span = pl.ds(pl.multiple_of(block * WIDTH, WIDTH), WIDTH)
        value = proj[span, :]
        gate = sigmoid(value)
        slope_in[span, :] = gate * (1.0 + value * (1.0 - gate))

    hot_ids = jnp.concatenate([id_recv[source, 0:1, :] for source in range(seqs)], axis=1)
    to_y, to_z = (hot_ids >> 6) & (ROUND - 1), hot_ids >> 8
    hot_ids = jnp.where(hot_ids < 0, -1, ((to_y * deep + to_z) << 6) | (hot_ids & 63))

    def hot_table(block):
        spot = pl.multiple_of(block * LEN, LEN)
        hits[pl.ds(spot, LEN), :] = jnp.where(iota((LEN, seqs * LEN), 0) + spot == hot_ids, 1.0, 0.0).astype(BF16)

    tables = hits.shape[0] // LEN
    pl.loop(0, tables // 2)(hot_table)
    ids.sent()
    ns.sent()
    remote(qkv_recv.at[others], qkv_recv.at[others], send_sem.at[0], qkv_rs.at[0], {"seq": me}).wait_send()

    def pooled(mean_of, spread_of, first_of, second_of):
        mean = sum(mean_of) * (1.0 / seqs)
        spread = sum(spread_of[head] + HEAD * (mean_of[head] - mean) ** 2 for head in range(seqs))
        inv = lax.rsqrt(spread * (1.0 / WIDTH) + EPS)
        first = sum(first_of) * (1.0 / WIDTH)
        second = sum(second_of[head] + (mean_of[head] - mean) * first_of[head] for head in range(seqs))
        return mean, inv, first, inv * second * (1.0 / WIDTH)

    def norms(part):
        stats[part].got()
        sums = [[stat_recv[part, head, pl.ds(kind * half, half), :] for head in range(seqs)] for kind in range(4)]
        own_mean = stat_send[part, pl.ds(0, half), :]
        return (own_mean,) + pooled(*sums)

    for block in reversed(range(seqs)):
        low = max(0, block - BAND)
        count = block + 1 - low
        if block % half == half - 1:
            norm = norms(block // half)
        own_mean, mean, inv, first, second = (array[block % half : block % half + 1, :] for array in norm)
        normed_here = (att[block] + (own_mean - mean)) * inv
        grad = (inv * (n_recv[block].astype(F32) - first - normed_here * second)).astype(BF16)
        query = qkv_recv[block, QUERY]
        span = pl.ds(low * LEN, count * LEN)
        grad_weight = mm(values[span, :], grad)
        grad_score = (grad_weight * slope[block, pl.ds(0, count * LEN), :]).astype(BF16)
        across = jnp.concatenate([qkv_recv[other, KEY] for other in range(low, block + 1)], axis=1)
        grad_value = mm_t(grad, weight[block, pl.ds(0, count * LEN), :])
        grad_key = mm_t(query, grad_score)
        dg_send[block, QUERY] = mm(across, grad_score).astype(BF16)
        for other in range(low, block + 1):
            cut = slice((other - low) * LEN, (other - low + 1) * LEN)
            new_value, new_key = grad_value[:, cut], grad_key[:, cut]
            if block < min(seqs - 1, other + BAND):
                new_value, new_key = new_value + dkv[other, 0], new_key + dkv[other, 1]
            if other == block:
                dg_send[block, VALUE] = new_value.astype(BF16)
                dg_send[block, KEY] = new_key.astype(BF16)
            else:
                dkv[other, 0] = new_value
                dkv[other, 1] = new_key

        @pl.when(block != me)
        def _():
            dg.start(dg_send.at[block], dg_recv.at[me], "seq", block)

    dg_recv[me] = dg_send[me]

    numy.got()
    for step in range(1, deep):
        peer = lax.rem(z + step, deep)
        numz.start(numy_recv, numz_recv.at[z], "tab", peer * ROUND + y)
    numz_recv[z] = numy_recv[...]

    pl.loop(tables // 2, tables)(hot_table)
    out_at, in_at = iota((LEN, LEN), 0), iota((LEN, LEN), 1)
    order = jnp.where(
        ((out_at >> 4) == ((in_at >> 1) & 7)) & (((out_at >> 1) & 7) == (in_at >> 4)) & ((out_at & 1) == (in_at & 1)), 1.0, 0.0
    ).astype(BF16)
    offs.got()
    sums = []
    for kind in range(4):
        spot = kind * half + lax.rem(me, half)
        sums.append([stat_recv[me // half, head, pl.ds(spot, 1), :] for head in range(seqs)])
    mean, inv, _, _ = pooled(*sums)
    for head in range(HEADS):
        span = pl.ds(head * HEAD, HEAD)
        normed_here = (off_recv[head].astype(F32) + (sums[0][head] - mean)) * inv
        gproj[span, :] = (gated[span, :] * normed_here * slope_in[span, :]).astype(BF16)
    grad_in = mm(w_ref[:, 0:WIDTH], gproj[0:WIDTH, :])
    for part in stats:
        part.sent()
    offs.sent()
    numy.sent()

    dg.got()
    for part in range(3):
        span = pl.ds((part + 1) * WIDTH, WIDTH)
        gproj[span, :] = (dg_recv[:, part].reshape(WIDTH, LEN).astype(F32) * slope_in[span, :]).astype(BF16)
    grad_in = grad_in + mm(w_ref[:, WIDTH:], gproj[WIDTH:, :])
    norm_in = xhat[...]
    grad_rows = og_ref[...].astype(F32).T + inv_in * (
        grad_in
        - jnp.mean(grad_in, axis=0, keepdims=True)
        - norm_in * jnp.mean(grad_in * norm_in, axis=0, keepdims=True)
    )
    grad_rows = grad_rows.astype(BF16)

    row_send[...] = grad_rows.reshape(row_send.shape)
    seq_all(row, lambda peer: row_send.at[peer], row_recv.at[me])
    row_recv[me] = row_send[me]

    for chunk in reversed(range(near, chunks)):
        packed[chunk] = mm_t(own_hits[chunk], grad_rows).astype(BF16).reshape(seqs, 2 * seqs, WIDTH)
        tab_chunk(along[chunk], chunk, lambda lane: packed.at[chunk, lane], tab_recv)
        if chunk == last:
            tab_recv[home] = packed[chunk, ROUND + y]
    for chunk in range(near):
        packed[chunk] = mm_t(own_hits[chunk], grad_rows).astype(BF16).reshape(seqs, 2 * seqs, WIDTH)
        for peer in range(seqs):
            near_send[peer, chunk] = packed[chunk, peer]
    if near:
        seq_all(cold, lambda peer: near_send.at[peer], near_recv.at[me])
        near_recv[me] = near_send[me]
    dg.sent()

    numz.got()
    for chunk in range(chunks):
        numbers = jnp.zeros((8, LEN), F32)
        lane_at = iota((8, LEN), 1) >> 4
        for lane in range(lanes):
            source = lax.rem(z + far_z(chunk, lane // ROUND) + deep, deep)
            tile = numz_recv[source, lane % ROUND].astype(F32)[:8]
            shift = lax.rem(2 * seqs * (lane - z) + LEN, LEN)
            numbers = jnp.where(lane_at == lane, pltpu.roll(tile, shift, 1), numbers)
        if chunk >= near:
            numbers = mm_t(numbers.astype(BF16), order)
        numbers = (16.0 * numbers[0:1, :] + numbers[1:2, :]).astype(I32)
        table[:, pl.ds(chunk * LEN, LEN)] = jnp.where(iota((cold_ref.shape[0], LEN), 0) == numbers, 1.0, 0.0).astype(BF16)
    numz.sent()

    row.got()
    slab = jnp.concatenate([row_recv[source] for source in range(seqs)], axis=1)
    slab = jnp.concatenate([slab, slab], axis=0)
    left = iota((share // 2, LEN), 1) < HEAD
    for step in range(ROUND):
        peer = lax.rem(y + 1 + step, ROUND)
        sums = mm_t(hits[pl.ds(pl.multiple_of(peer * deep * share, deep * share), deep * share), :], slab)
        for plane in range(deep):
            first = plane * share
            upper, lower = sums[first : first + share // 2], sums[first + share // 2 : first + share]
            hoty_send[peer, plane] = jnp.where(left, upper, lower).astype(BF16)
        if step < ROUND - 1:
            hoty.start(hoty_send.at[peer], hoty_recv.at[y], "tab", z * ROUND + peer)
    hoty_recv[y] = hoty_send[y]

    if near:
        cold.got()
    for chunk in reversed(range(near)):
        rows = mm(order, near_recv[:, chunk].reshape(LEN, WIDTH)).astype(BF16)
        tab_send[chunk] = rows.reshape(lanes, 2 * seqs, WIDTH)
        tab_chunk(along[chunk], chunk, lambda lane: tab_send.at[chunk, lane], tab_recv)
        if chunk == last:
            tab_recv[home] = tab_send[chunk, ROUND + y]

    hoty.got()
    for plane in range(deep):
        sums = sum(hoty_recv[source, plane].astype(F32) for source in range(ROUND))
        hotz_send[plane] = sums.astype(BF16)
    for step in range(1, deep):
        peer = lax.rem(z + step, deep)
        hotz.start(hotz_send.at[peer], hotz_recv.at[z], "tab", peer * ROUND + y)
    hotz_recv[z] = hotz_send[z]

    for chunk in reversed(range(near, chunks)):
        along[chunk].got()
        rows = mm(order, tab_recv[pl.ds(chunk * lanes, lanes)].reshape(LEN, WIDTH)).astype(BF16)
        far_send[chunk - near] = rows.reshape(seqs, 2 * lanes, WIDTH)
        seq_all(back[chunk - near], lambda peer: far_send.at[chunk - near, peer], far_recv.at[chunk - near, me])
        far_recv[chunk - near, me] = far_send[chunk - near, me]

    hotz.got()
    sum_send[...] = sum(hotz_recv[source].astype(F32) for source in range(deep)).astype(BF16)
    seq_all(total, lambda peer: sum_send, sum_recv.at[me])
    sum_recv[me] = sum_send[...]
    row.sent()
    hoty.sent()
    hotz.sent()
    if near:
        cold.sent()
    for chunk in range(near, chunks):
        along[chunk].sent()

    for chunk in range(near):
        along[chunk].got()
    result = jnp.zeros(cold_ref.shape, F32)
    if near:
        result = mm(table[:, : near * LEN], tab_recv[0 : near * lanes].reshape(near * LEN, WIDTH))
    for part in back:
        part.got()
    if near < chunks:
        result = result + mm(table[:, near * LEN :], far_recv[...].reshape((chunks - near) * LEN, WIDTH))
    cold_ref[...] = result

    total.got()
    for pair in range(seqs // 2):
        even, odd = sum_recv[2 * pair].astype(F32), sum_recv[2 * pair + 1].astype(F32)
        span = pl.ds(pair * LEN, LEN)
        hot_ref[0 : share // 2, span] = jnp.where(left, even, pltpu.roll(odd, HEAD, 1))
        hot_ref[share // 2 :, span] = jnp.where(left, pltpu.roll(even, HEAD, 1), odd)

    finish()


def solution(mesh):
    seqs, tabs = mesh.shape["seq"], mesh.shape["tab"]
    deep = tabs // ROUND
    chunks = deep // 2
    near = NEAR if NEAR is not None else chunks // 2
    lanes = 2 * ROUND
    group = seqs * LEN
    inputs = [
        pltpu.VMEM((LEN, WIDTH), BF16),
        pltpu.VMEM((LEN, WIDTH), BF16),
        pltpu.SMEM((1, 4), I32),
        pltpu.VMEM((1, LEN), I32),
        pltpu.VMEM((1, LEN), I32),
        pltpu.VMEM((1, LEN), I32),
        pltpu.VMEM((1, LEN), I32),
        pltpu.VMEM((WIDTH, 4 * WIDTH), BF16),
        pltpu.VMEM((WIDTH, WIDTH), BF16),
        pltpu.SemaphoreType.DMA((10,)),
    ]
    exchanged = [
        pltpu.VMEM((HEADS, 3, HEAD, LEN), BF16),
        pltpu.VMEM((seqs, 3, HEAD, LEN), BF16),
        pltpu.VMEM((HEADS, HEAD, LEN), BF16),
        pltpu.VMEM((seqs, HEAD, LEN), BF16),
        pltpu.VMEM((8, LEN), I32),
        pltpu.VMEM((seqs, 8, LEN), I32),
        pltpu.VMEM((2, 2 * seqs, LEN), F32),
        pltpu.VMEM((2, seqs, 2 * seqs, LEN), F32),
        pltpu.VMEM((seqs, HEAD, LEN), BF16),
        pltpu.VMEM((HEADS, HEAD, LEN), BF16),
        pltpu.VMEM((seqs, 3, HEAD, LEN), BF16),
        pltpu.VMEM((HEADS, 3, HEAD, LEN), BF16),
        pltpu.VMEM((seqs, HEAD, LEN), BF16),
        pltpu.VMEM((seqs, HEAD, LEN), BF16),
        pltpu.VMEM((seqs, max(near, 1), 2 * lanes, WIDTH), BF16),
        pltpu.VMEM((seqs, max(near, 1), 2 * lanes, WIDTH), BF16),
        pltpu.VMEM((max(near, 1), lanes, 2 * seqs, WIDTH), BF16),
        pltpu.VMEM((tabs, 2 * seqs, WIDTH), BF16),
        pltpu.VMEM((max(chunks - near, 1), seqs, 2 * lanes, WIDTH), BF16),
        pltpu.VMEM((max(chunks - near, 1), seqs, 2 * lanes, WIDTH), BF16),
        pltpu.VMEM((ROUND, 2 * seqs, LEN), BF16),
        pltpu.VMEM((ROUND, 2 * seqs, LEN), BF16),
        pltpu.VMEM((deep, ROUND, 2 * seqs, LEN), BF16),
        pltpu.VMEM((ROUND, deep, HEAD // 2, LEN), BF16),
        pltpu.VMEM((ROUND, deep, HEAD // 2, LEN), BF16),
        pltpu.VMEM((deep, HEAD // 2, LEN), BF16),
        pltpu.VMEM((deep, HEAD // 2, LEN), BF16),
        pltpu.VMEM((HEAD // 2, LEN), BF16),
        pltpu.VMEM((seqs, HEAD // 2, LEN), BF16),
    ]
    band = (BAND + 1) * LEN
    work = [
        pltpu.VMEM((4 * WIDTH, LEN), F32),
        pltpu.VMEM((4 * WIDTH, LEN), F32),
        pltpu.VMEM((WIDTH, LEN), F32),
        pltpu.VMEM((WIDTH, LEN), F32),
        pltpu.VMEM((group, HEAD), BF16),
        pltpu.VMEM((group, HEAD), BF16),
        pltpu.VMEM((seqs, band, LEN), BF16),
        pltpu.VMEM((seqs, band, LEN), F32),
        pltpu.VMEM((seqs, HEAD, LEN), F32),
        pltpu.VMEM((seqs, 2, HEAD, LEN), F32),
        pltpu.VMEM((4 * WIDTH, LEN), BF16),
        pltpu.VMEM((64 * tabs, group), BF16),
        pltpu.VMEM((chunks, LEN, LEN), BF16),
        pltpu.VMEM((chunks, seqs, 2 * seqs, WIDTH), BF16),
        pltpu.VMEM((512, chunks * LEN), BF16),
    ]
    dma = pltpu.SemaphoreType.DMA
    sems = [dma((13,)), dma((13,)), dma((seqs,))] + [dma((chunks,)) for _ in range(6)]

    def local(history_rows, out_grad, seg_lengths, hot_flag, hot_slot, cold_owner, cold_row, input_weight, w_out):
        vmem = pl.BlockSpec(memory_space=pltpu.VMEM)
        return pl.pallas_call(
            functools.partial(kernel, seqs, tabs),
            out_shape=(
                jax.ShapeDtypeStruct((512, WIDTH), F32),
                jax.ShapeDtypeStruct((64, WIDTH), F32),
            ),
            in_specs=[pl.BlockSpec(memory_space=pltpu.HBM)] * 9,
            out_specs=(vmem, vmem),
            scratch_shapes=inputs + exchanged + work + sems,
            compiler_params=pltpu.CompilerParams(
                collective_id=0, has_side_effects=True, vmem_limit_bytes=56 * 1024 * 1024
            ),
        )(
            history_rows.reshape(LEN, WIDTH),
            out_grad.reshape(LEN, WIDTH),
            seg_lengths,
            hot_flag,
            hot_slot,
            cold_owner.reshape(1, LEN),
            cold_row,
            input_weight,
            w_out,
        )

    in_specs = (
        P("tab", "seq", None),
        P("tab", "seq", None),
        P("tab", None),
        P("tab", "seq"),
        P("tab", "seq"),
        P("tab", "seq", None),
        P("tab", "seq"),
        P(),
        P(),
    )
    out_specs = (P(("seq", "tab"), None), P("tab", None))
    return jax.shard_map(local, mesh=mesh, in_specs=in_specs, out_specs=out_specs, check_vma=False)
```

```python
import functools

import jax
import jax.numpy as jnp
from jax import lax
from jax.experimental import pallas as pl
from jax.experimental.pallas import tpu as pltpu
from jax.sharding import PartitionSpec as P

HEADS = 8
HEAD = 64
LEN = 128
WIDTH = 512
BAND = 4
EPS = 1e-05
MESH = pl.DeviceIdType.MESH
F32 = jnp.float32
BF16 = jnp.bfloat16
I32 = jnp.int32
VALUE, QUERY, KEY = 0, 1, 2
ROUND = 4
NEAR = None


def mm(a, b):
    return jnp.dot(a, b, preferred_element_type=F32)


def mm_t(a, b):
    return lax.dot_general(a, b, (((1,), (1,)), ((), ())), preferred_element_type=F32)


def sigmoid(v):
    return 0.5 * jnp.tanh(0.5 * v) + 0.5


def iota(shape, dim):
    return lax.broadcasted_iota(I32, shape, dim)


def kernel(
    seqs, tabs,
    x_hbm, og_hbm, seg_hbm, flag_hbm, slot_hbm, owner_hbm, row_hbm, w_hbm, wo_hbm,
    cold_ref, hot_ref,
    x_ref, og_ref, seg_ref, flag_ref, slot_ref, owner_ref, row_ref, w_ref, wo_ref, in_sem,
    qkv_send, qkv_recv, n_send, n_recv, id_send, id_recv, stat_send, stat_recv, off_send, off_recv, dg_send, dg_recv,
    row_send, row_recv, near_send, near_recv, tab_send, tab_recv, far_send, far_recv, numy_send, numy_recv, numz_recv,
    hoty_send, hoty_recv, hotz_send, hotz_recv, sum_send, sum_recv,
    proj, slope_in, xhat, straight, gated, keys, values, weight, slope, att, dkv, gproj, hits, own_hits, packed, table,
    send_sem, recv_sem, qkv_rs, cold_ss, cold_rs, tab_ss, tab_rs, far_ss, far_rs,
):
    me = lax.axis_index("seq")
    tab = lax.axis_index("tab")
    deep = tabs // ROUND
    z, y = tab // ROUND, lax.rem(tab, ROUND)
    chunks = deep // 2
    last = chunks - 1
    near = NEAR if NEAR is not None else chunks // 2
    lanes = 2 * ROUND
    share = 64

    def far_z(chunk, side):
        if isinstance(chunk, int):
            return deep // 2 * (1 - side) if chunk == last else (chunk + 1) * (1 - 2 * side)
        return jnp.where(chunk == last, deep // 2 * (1 - side), (chunk + 1) * (1 - 2 * side))

    def tab_peer(chunk, lane):
        return lax.rem(z + far_z(chunk, lane // ROUND) + deep, deep) * ROUND + lax.rem(lane, ROUND)

    def tab_slot(chunk, lane):
        side = lane // ROUND
        return chunk * lanes + (side if chunk == last else 1 - side) * ROUND + y

    def remote(src, dst, ss, rs, peer):
        return pltpu.make_async_remote_copy(
            src_ref=src, dst_ref=dst, send_sem=ss, recv_sem=rs, device_id=peer, device_id_type=MESH
        )

    begun = []

    class Exchange:
        def __init__(self, ss, rs, sizing):
            self.ss, self.rs, self.sizing = ss, rs, sizing
            self.left = {"sent", "got"}

        def start(self, src, dst, axis, peer):
            if self not in begun:
                begun.append(self)
            remote(src, dst, self.ss, self.rs, {axis: peer}).start()

        def sent(self):
            self.left.discard("sent")
            remote(self.sizing, self.sizing, self.ss, self.rs, {"seq": me}).wait_send()

        def got(self):
            self.left.discard("got")
            remote(self.sizing, self.sizing, self.ss, self.rs, {"seq": me}).wait_recv()

    def finish():
        for one in begun:
            for name in sorted(one.left):
                getattr(one, name)()

    def seq_all(exchange, out, into):
        for step in range(1, seqs):
            peer = lax.rem(me + step, seqs)
            exchange.start(out(peer), into, "seq", peer)

    def tab_chunk(exchange, chunk, out, into):
        def one(lane):
            exchange.start(out(lane), into.at[tab_slot(chunk, lane)], "tab", tab_peer(chunk, lane))

        if chunk == last:
            pl.loop(0, ROUND)(one)

            @pl.loop(1, ROUND)
            def _(step):
                one(ROUND + lax.rem(y + step, ROUND))
        else:
            pl.loop(0, lanes)(one)

    home = last * lanes + ROUND + y

    def tab_sizing(into, chunk):
        return into.at[pl.ds(chunk * lanes, lanes - 1 if chunk == last else lanes)]

    others = pl.ds(0, seqs - 1)
    ns = Exchange(send_sem.at[1], recv_sem.at[1], n_recv.at[others])
    ids = Exchange(send_sem.at[2], recv_sem.at[2], id_recv.at[others])
    stats = [Exchange(send_sem.at[3 + half], recv_sem.at[3 + half], stat_recv.at[half, others]) for half in range(2)]
    offs = Exchange(send_sem.at[5], recv_sem.at[5], off_recv.at[others])
    dg = Exchange(send_sem.at[6], recv_sem.at[6], dg_recv.at[others])
    row = Exchange(send_sem.at[7], recv_sem.at[7], row_recv.at[others])
    numy = Exchange(send_sem.at[8], recv_sem.at[8], numy_recv.at[pl.ds(0, ROUND - 1)])
    numz = Exchange(send_sem.at[9], recv_sem.at[9], numz_recv.at[pl.ds(0, deep - 1)])
    hoty = Exchange(send_sem.at[10], recv_sem.at[10], hoty_recv.at[pl.ds(0, ROUND - 1)])
    hotz = Exchange(send_sem.at[11], recv_sem.at[11], hotz_recv.at[pl.ds(0, deep - 1)])
    total = Exchange(send_sem.at[12], recv_sem.at[12], sum_recv.at[others])
    cold = Exchange(cold_ss.at[0], cold_rs.at[0], near_recv.at[others])
    along = [Exchange(tab_ss.at[c], tab_rs.at[c], tab_sizing(tab_recv, c)) for c in range(chunks)]
    back = [Exchange(far_ss.at[c], far_rs.at[c], far_recv.at[c, others]) for c in range(chunks - near)]

    loads = [
        pltpu.make_async_copy(src, dst, in_sem.at[index])
        for index, (src, dst) in enumerate(
            (
                (flag_hbm, flag_ref),
                (slot_hbm, slot_ref),
                (owner_hbm, owner_ref),
                (row_hbm, row_ref),
                (x_hbm, x_ref),
                (w_hbm.at[:, pl.ds(WIDTH, 3 * WIDTH)], w_ref.at[:, pl.ds(WIDTH, 3 * WIDTH)]),
                (seg_hbm, seg_ref),
                (og_hbm, og_ref),
                (wo_hbm, wo_ref),
                (w_hbm.at[:, pl.ds(0, WIDTH)], w_ref.at[:, pl.ds(0, WIDTH)]),
            )
        )
    ]
    for load in loads:
        load.start()

    barrier = pltpu.get_barrier_semaphore()
    for step in range(1, seqs):
        pl.semaphore_signal(barrier, inc=1, device_id={"seq": lax.rem(me + step, seqs)}, device_id_type=MESH)

    for step in range(1, ROUND):
        peer = z * ROUND + lax.rem(y + step, ROUND)
        pl.semaphore_signal(barrier, inc=1, device_id={"tab": peer}, device_id_type=MESH)
    for step in range(1, deep):
        peer = lax.rem(z + step, deep) * ROUND + y
        pl.semaphore_signal(barrier, inc=1, device_id={"tab": peer}, device_id_type=MESH)

    for load in loads[:4]:
        load.wait()
    flag = flag_ref[...]
    owner = jnp.where(flag == 1, -1, owner_ref[...])
    owner_row = jnp.broadcast_to(owner.astype(F32), (LEN, LEN))
    earlier = (owner_row.T == owner_row) & (iota((LEN, LEN), 0) < iota((LEN, LEN), 1))
    taken = jnp.sum(jnp.where(earlier, 1.0, 0.0), axis=0, keepdims=True)
    lane_of = jnp.where(flag == 1, -1, owner * 2 + taken.astype(I32))
    which = iota((8, LEN), 0)
    id_send[...] = jnp.where(
        which == 0,
        jnp.where(flag == 1, slot_ref[...], -1),
        jnp.where(which == 1, lane_of, jnp.where(which == 2, row_ref[...], 0)),
    )
    id_recv[me] = id_send[...]

    loads[4].wait()
    wide = x_ref[...].astype(F32)
    centered = wide - jnp.mean(wide, axis=1, keepdims=True)
    normed = centered * lax.rsqrt(jnp.mean(centered * centered, axis=1, keepdims=True) + EPS)
    xin = normed.astype(BF16)

    def project(block, pair):
        spot = pl.multiple_of(block * WIDTH + pair * LEN, LEN)
        out = mm(xin, w_ref[:, pl.ds(spot, LEN)]).T
        proj[pl.ds(spot, LEN), :] = out
        return (out * sigmoid(out)).astype(BF16).reshape(2, HEAD, LEN)

    def qkv_copy(peer):
        return remote(qkv_send.at[peer], qkv_recv.at[me], send_sem.at[0], qkv_rs.at[me], {"seq": peer})

    loads[5].wait()
    pairs = [lax.rem(me // 2 + 1 + step, HEADS // 2) for step in range(HEADS // 2)]
    for pair in pairs:
        for part, block in ((VALUE, 1), (QUERY, 2), (KEY, 3)):
            qkv_send[pl.ds(2 * pair, 2), part] = project(block, pair)
    pl.semaphore_wait(barrier, seqs - 1 + ROUND - 1 + deep - 1)
    for pair in pairs:
        for core in range(2):
            peer = 2 * pair + core

            @pl.when(peer != me)
            def _():
                qkv_copy(peer).start()

    qkv_recv[me] = qkv_send[me]

    for load in loads[6:]:
        load.wait()
    for pair in pairs:
        spot = pl.multiple_of(pair * LEN, LEN)
        up = mm_t(wo_ref[pl.ds(spot, LEN), :], og_ref[...])
        gated[pl.ds(spot, LEN), :] = up
        n_send[pl.ds(2 * pair, 2)] = (up.reshape(2, HEAD, LEN) * project(0, pair).astype(F32)).astype(BF16)
    n_recv[me] = n_send[me]

    for chunk in range(chunks):
        place = iota((lanes * 2 * seqs, LEN), 0)
        major, minor = place >> 4, (place >> 1) & 7
        to_seq, lane = (major, minor) if chunk < near else (minor, major)
        wanted = (to_seq * tabs + tab_peer(chunk, lane)) * 2 + (place & 1)
        own_hits[chunk] = jnp.where(wanted == id_send[1:2, :], 1.0, 0.0).astype(BF16)

    end0 = seg_ref[0, 0]
    end1 = end0 + seg_ref[0, 1]
    end2 = end1 + seg_ref[0, 2]
    for step in range(HEADS // 2):
        for core in range(2):
            source = 2 * lax.rem(me // 2 + 3 - step + HEADS // 2, HEADS // 2) + core

            @pl.when(source != me)
            def _():
                slab = qkv_recv.at[source]
                remote(slab, slab, send_sem.at[0], qkv_rs.at[source], {"seq": me}).wait_recv()

            span = pl.ds(pl.multiple_of(source * LEN, LEN), LEN)
            keys[span, :] = qkv_recv[source, KEY].astype(F32).T.astype(BF16)
            values[span, :] = qkv_recv[source, VALUE].astype(F32).T.astype(BF16)
        if step == 0:
            seq_all(ns, lambda peer: n_send.at[peer], n_recv.at[me])
            seq_all(ids, lambda peer: id_send, id_recv.at[me])

    half = seqs // 2
    for block in reversed(range(seqs)):
        low = max(0, block - BAND)
        count = block + 1 - low
        score = mm(keys[pl.ds(low * LEN, count * LEN), :], qkv_recv[block, QUERY]) * 0.125
        here = block * LEN + iota((1, LEN), 1)
        start = jnp.where(here >= end2, end2, jnp.where(here >= end1, end1, jnp.where(here >= end0, end0, 0)))
        there = low * LEN + iota(score.shape, 0)
        allowed = (there >= start) & (there <= here)
        gate = sigmoid(score)
        swish = score * gate
        heavy = jnp.where(allowed, swish, 0.0).astype(BF16)
        weight[block, pl.ds(0, count * LEN), :] = heavy
        slope[block, pl.ds(0, count * LEN), :] = jnp.where(allowed, (gate + swish * (1.0 - gate)) * 0.125, 0.0)
        across = jnp.concatenate([qkv_recv[other, VALUE] for other in range(low, block + 1)], axis=1)
        mixed = mm(across, heavy)
        if block == seqs - 1:
            ns.got()
        grad = n_recv[block].astype(F32)
        mean = jnp.mean(mixed, axis=0, keepdims=True)
        off = mixed - mean
        att[block] = off
        off_send[block] = off.astype(BF16)
        part, line = block // half, block % half
        for kind, sums in enumerate(
            (
                mean,
                jnp.sum(off * off, axis=0, keepdims=True),
                jnp.sum(grad, axis=0, keepdims=True),
                jnp.sum(grad * off, axis=0, keepdims=True),
            )
        ):
            stat_send[part, pl.ds(kind * half + line, 1), :] = sums
        if line == 0:
            seq_all(stats[part], lambda peer: stat_send.at[part], stat_recv.at[part, me])
            stat_recv[part, me] = stat_send[part]
    seq_all(offs, lambda peer: off_send.at[peer], off_recv.at[me])
    off_recv[me] = off_send[me]

    ids.got()
    place = iota((LEN, LEN), 0)
    for step in range(ROUND):
        peer = lax.rem(y + 1 + step, ROUND)
        wanted = (me * tabs + (place >> 4) * ROUND + peer) * 2 + (place & 1)
        numbers = jnp.zeros((2 * seqs, LEN), F32)
        for source in range(seqs):
            mine = jnp.where(((place >> 1) & (seqs - 1)) == source, wanted, -5)
            pick = jnp.where(mine == id_recv[source, 1:2, :], 1.0, 0.0).astype(BF16)
            number = id_recv[source, 2:3, :]
            line = iota((2 * seqs, LEN), 0)
            halves = jnp.where(line == 0, number >> 4, jnp.where(line == 1, number & 15, 0))
            numbers = numbers + mm_t(halves.astype(F32).astype(BF16), pick)
        numy_send[peer] = numbers.astype(BF16)
        if step < ROUND - 1:
            numy.start(numy_send.at[peer], numy_recv.at[y], "tab", z * ROUND + peer)
    numy_recv[y] = numy_send[y]

    across = x_ref[...].astype(F32).T
    across = across - jnp.mean(across, axis=0, keepdims=True)
    inv_in = lax.rsqrt(jnp.mean(across * across, axis=0, keepdims=True) + EPS)
    xhat[...] = across * inv_in
    straight[...] = og_ref[...].astype(F32).T

    @pl.loop(0, 4)
    def _(block):
        span = pl.ds(pl.multiple_of(block * WIDTH, WIDTH), WIDTH)
        value = proj[span, :]
        gate = sigmoid(value)
        slope_in[span, :] = gate * (1.0 + value * (1.0 - gate))

    hot_ids = jnp.concatenate([id_recv[source, 0:1, :] for source in range(seqs)], axis=1)
    to_y, to_z = (hot_ids >> 6) & (ROUND - 1), hot_ids >> 8
    hot_ids = jnp.where(hot_ids < 0, -1, ((to_y * deep + to_z) << 6) | (hot_ids & 63))

    def hot_table(block):
        spot = pl.multiple_of(block * LEN, LEN)
        hits[pl.ds(spot, LEN), :] = jnp.where(iota((LEN, seqs * LEN), 0) + spot == hot_ids, 1.0, 0.0).astype(BF16)

    tables = hits.shape[0] // LEN
    pl.loop(0, tables // 2)(hot_table)
    ids.sent()
    ns.sent()
    remote(qkv_recv.at[others], qkv_recv.at[others], send_sem.at[0], qkv_rs.at[0], {"seq": me}).wait_send()

    def pooled(mean_of, spread_of, first_of, second_of):
        mean = sum(mean_of) * (1.0 / seqs)
        spread = sum(spread_of[head] + HEAD * (mean_of[head] - mean) ** 2 for head in range(seqs))
        inv = lax.rsqrt(spread * (1.0 / WIDTH) + EPS)
        first = sum(first_of) * (1.0 / WIDTH)
        second = sum(second_of[head] + (mean_of[head] - mean) * first_of[head] for head in range(seqs))
        return mean, inv, first, inv * second * (1.0 / WIDTH)

    def norms(part):
        stats[part].got()
        sums = [[stat_recv[part, head, pl.ds(kind * half, half), :] for head in range(seqs)] for kind in range(4)]
        own_mean = stat_send[part, pl.ds(0, half), :]
        return (own_mean,) + pooled(*sums)

    for block in reversed(range(seqs)):
        low = max(0, block - BAND)
        count = block + 1 - low
        if block % half == half - 1:
            norm = norms(block // half)
        own_mean, mean, inv, first, second = (array[block % half : block % half + 1, :] for array in norm)
        normed_here = (att[block] + (own_mean - mean)) * inv
        grad = (inv * (n_recv[block].astype(F32) - first - normed_here * second)).astype(BF16)
        query = qkv_recv[block, QUERY]
        span = pl.ds(low * LEN, count * LEN)
        grad_weight = mm(values[span, :], grad)
        grad_score = (grad_weight * slope[block, pl.ds(0, count * LEN), :]).astype(BF16)
        across = jnp.concatenate([qkv_recv[other, KEY] for other in range(low, block + 1)], axis=1)
        grad_value = mm_t(grad, weight[block, pl.ds(0, count * LEN), :])
        grad_key = mm_t(query, grad_score)
        dg_send[block, QUERY] = mm(across, grad_score).astype(BF16)
        for other in range(low, block + 1):
            cut = slice((other - low) * LEN, (other - low + 1) * LEN)
            new_value, new_key = grad_value[:, cut], grad_key[:, cut]
            if block < min(seqs - 1, other + BAND):
                new_value, new_key = new_value + dkv[other, 0], new_key + dkv[other, 1]
            if other == block:
                dg_send[block, VALUE] = new_value.astype(BF16)
                dg_send[block, KEY] = new_key.astype(BF16)
            else:
                dkv[other, 0] = new_value
                dkv[other, 1] = new_key

        @pl.when(block != me)
        def _():
            dg.start(dg_send.at[block], dg_recv.at[me], "seq", block)

    dg_recv[me] = dg_send[me]

    numy.got()
    for step in range(1, deep):
        peer = lax.rem(z + step, deep)
        numz.start(numy_recv, numz_recv.at[z], "tab", peer * ROUND + y)
    numz_recv[z] = numy_recv[...]

    pl.loop(tables // 2, tables)(hot_table)
    out_at, in_at = iota((LEN, LEN), 0), iota((LEN, LEN), 1)
    order = jnp.where(
        ((out_at >> 4) == ((in_at >> 1) & 7)) & (((out_at >> 1) & 7) == (in_at >> 4)) & ((out_at & 1) == (in_at & 1)), 1.0, 0.0
    ).astype(BF16)
    offs.got()
    sums = []
    for kind in range(4):
        spot = kind * half + lax.rem(me, half)
        sums.append([stat_recv[me // half, head, pl.ds(spot, 1), :] for head in range(seqs)])
    mean, inv, _, _ = pooled(*sums)
    for head in range(HEADS):
        span = pl.ds(head * HEAD, HEAD)
        normed_here = (off_recv[head].astype(F32) + (sums[0][head] - mean)) * inv
        gproj[span, :] = (gated[span, :] * normed_here * slope_in[span, :]).astype(BF16)
    grad_in = mm(w_ref[:, 0:WIDTH], gproj[0:WIDTH, :])
    for part in stats:
        part.sent()
    offs.sent()
    numy.sent()

    dg.got()
    for part in range(3):
        span = pl.ds((part + 1) * WIDTH, WIDTH)
        gproj[span, :] = (dg_recv[:, part].reshape(WIDTH, LEN).astype(F32) * slope_in[span, :]).astype(BF16)
    grad_in = grad_in + mm(w_ref[:, WIDTH:], gproj[WIDTH:, :])
    norm_in = xhat[...]
    grad_rows = straight[...] + inv_in * (
        grad_in
        - jnp.mean(grad_in, axis=0, keepdims=True)
        - norm_in * jnp.mean(grad_in * norm_in, axis=0, keepdims=True)
    )
    grad_rows = grad_rows.astype(BF16)

    row_send[...] = grad_rows.reshape(row_send.shape)
    seq_all(row, lambda peer: row_send.at[peer], row_recv.at[me])
    row_recv[me] = row_send[me]

    for chunk in reversed(range(near, chunks)):
        packed[chunk] = mm_t(own_hits[chunk], grad_rows).astype(BF16).reshape(seqs, 2 * seqs, WIDTH)
        tab_chunk(along[chunk], chunk, lambda lane: packed.at[chunk, lane], tab_recv)
        if chunk == last:
            tab_recv[home] = packed[chunk, ROUND + y]
    for chunk in range(near):
        packed[chunk] = mm_t(own_hits[chunk], grad_rows).astype(BF16).reshape(seqs, 2 * seqs, WIDTH)
        for peer in range(seqs):
            near_send[peer, chunk] = packed[chunk, peer]
    if near:
        seq_all(cold, lambda peer: near_send.at[peer], near_recv.at[me])
        near_recv[me] = near_send[me]
    dg.sent()

    numz.got()
    for chunk in range(chunks):
        numbers = jnp.zeros((8, LEN), F32)
        lane_at = iota((8, LEN), 1) >> 4
        for lane in range(lanes):
            source = lax.rem(z + far_z(chunk, lane // ROUND) + deep, deep)
            tile = numz_recv[source, lane % ROUND].astype(F32)[:8]
            shift = lax.rem(2 * seqs * (lane - z) + LEN, LEN)
            numbers = jnp.where(lane_at == lane, pltpu.roll(tile, shift, 1), numbers)
        if chunk >= near:
            numbers = mm_t(numbers.astype(BF16), order)
        numbers = (16.0 * numbers[0:1, :] + numbers[1:2, :]).astype(I32)
        table[:, pl.ds(chunk * LEN, LEN)] = jnp.where(iota((cold_ref.shape[0], LEN), 0) == numbers, 1.0, 0.0).astype(BF16)
    numz.sent()

    row.got()
    slab = jnp.concatenate([row_recv[source] for source in range(seqs)], axis=1)
    slab = jnp.concatenate([slab, slab], axis=0)
    left = iota((share // 2, LEN), 1) < HEAD
    for step in range(ROUND):
        peer = lax.rem(y + 1 + step, ROUND)
        sums = mm_t(hits[pl.ds(pl.multiple_of(peer * deep * share, deep * share), deep * share), :], slab)
        for plane in range(deep):
            first = plane * share
            upper, lower = sums[first : first + share // 2], sums[first + share // 2 : first + share]
            hoty_send[peer, plane] = jnp.where(left, upper, lower).astype(BF16)
        if step < ROUND - 1:
            hoty.start(hoty_send.at[peer], hoty_recv.at[y], "tab", z * ROUND + peer)
    hoty_recv[y] = hoty_send[y]

    if near:
        cold.got()
    for chunk in reversed(range(near)):
        rows = mm(order, near_recv[:, chunk].reshape(LEN, WIDTH)).astype(BF16)
        tab_send[chunk] = rows.reshape(lanes, 2 * seqs, WIDTH)
        tab_chunk(along[chunk], chunk, lambda lane: tab_send.at[chunk, lane], tab_recv)
        if chunk == last:
            tab_recv[home] = tab_send[chunk, ROUND + y]

    hoty.got()
    for plane in range(deep):
        sums = sum(hoty_recv[source, plane].astype(F32) for source in range(ROUND))
        hotz_send[plane] = sums.astype(BF16)
    for step in range(1, deep):
        peer = lax.rem(z + step, deep)
        hotz.start(hotz_send.at[peer], hotz_recv.at[z], "tab", peer * ROUND + y)
    hotz_recv[z] = hotz_send[z]

    for chunk in reversed(range(near, chunks)):
        along[chunk].got()
        rows = mm(order, tab_recv[pl.ds(chunk * lanes, lanes)].reshape(LEN, WIDTH)).astype(BF16)
        far_send[chunk - near] = rows.reshape(seqs, 2 * lanes, WIDTH)
        seq_all(back[chunk - near], lambda peer: far_send.at[chunk - near, peer], far_recv.at[chunk - near, me])
        far_recv[chunk - near, me] = far_send[chunk - near, me]

    hotz.got()
    sum_send[...] = sum(hotz_recv[source].astype(F32) for source in range(deep)).astype(BF16)
    seq_all(total, lambda peer: sum_send, sum_recv.at[me])
    sum_recv[me] = sum_send[...]
    row.sent()
    hoty.sent()
    hotz.sent()
    if near:
        cold.sent()
    for chunk in range(near, chunks):
        along[chunk].sent()

    for chunk in range(near):
        along[chunk].got()
    result = jnp.zeros(cold_ref.shape, F32)
    if near:
        result = mm(table[:, : near * LEN], tab_recv[0 : near * lanes].reshape(near * LEN, WIDTH))
    for part in back:
        part.got()
    if near < chunks:
        result = result + mm(table[:, near * LEN :], far_recv[...].reshape((chunks - near) * LEN, WIDTH))
    cold_ref[...] = result

    total.got()
    for pair in range(seqs // 2):
        even, odd = sum_recv[2 * pair].astype(F32), sum_recv[2 * pair + 1].astype(F32)
        span = pl.ds(pair * LEN, LEN)
        hot_ref[0 : share // 2, span] = jnp.where(left, even, pltpu.roll(odd, HEAD, 1))
        hot_ref[share // 2 :, span] = jnp.where(left, pltpu.roll(even, HEAD, 1), odd)

    finish()


def solution(mesh):
    seqs, tabs = mesh.shape["seq"], mesh.shape["tab"]
    deep = tabs // ROUND
    chunks = deep // 2
    near = NEAR if NEAR is not None else chunks // 2
    lanes = 2 * ROUND
    group = seqs * LEN
    inputs = [
        pltpu.VMEM((LEN, WIDTH), BF16),
        pltpu.VMEM((LEN, WIDTH), BF16),
        pltpu.SMEM((1, 4), I32),
        pltpu.VMEM((1, LEN), I32),
        pltpu.VMEM((1, LEN), I32),
        pltpu.VMEM((1, LEN), I32),
        pltpu.VMEM((1, LEN), I32),
        pltpu.VMEM((WIDTH, 4 * WIDTH), BF16),
        pltpu.VMEM((WIDTH, WIDTH), BF16),
        pltpu.SemaphoreType.DMA((10,)),
    ]
    exchanged = [
        pltpu.VMEM((HEADS, 3, HEAD, LEN), BF16),
        pltpu.VMEM((seqs, 3, HEAD, LEN), BF16),
        pltpu.VMEM((HEADS, HEAD, LEN), BF16),
        pltpu.VMEM((seqs, HEAD, LEN), BF16),
        pltpu.VMEM((8, LEN), I32),
        pltpu.VMEM((seqs, 8, LEN), I32),
        pltpu.VMEM((2, 2 * seqs, LEN), F32),
        pltpu.VMEM((2, seqs, 2 * seqs, LEN), F32),
        pltpu.VMEM((seqs, HEAD, LEN), BF16),
        pltpu.VMEM((HEADS, HEAD, LEN), BF16),
        pltpu.VMEM((seqs, 3, HEAD, LEN), BF16),
        pltpu.VMEM((HEADS, 3, HEAD, LEN), BF16),
        pltpu.VMEM((seqs, HEAD, LEN), BF16),
        pltpu.VMEM((seqs, HEAD, LEN), BF16),
        pltpu.VMEM((seqs, max(near, 1), 2 * lanes, WIDTH), BF16),
        pltpu.VMEM((seqs, max(near, 1), 2 * lanes, WIDTH), BF16),
        pltpu.VMEM((max(near, 1), lanes, 2 * seqs, WIDTH), BF16),
        pltpu.VMEM((tabs, 2 * seqs, WIDTH), BF16),
        pltpu.VMEM((max(chunks - near, 1), seqs, 2 * lanes, WIDTH), BF16),
        pltpu.VMEM((max(chunks - near, 1), seqs, 2 * lanes, WIDTH), BF16),
        pltpu.VMEM((ROUND, 2 * seqs, LEN), BF16),
        pltpu.VMEM((ROUND, 2 * seqs, LEN), BF16),
        pltpu.VMEM((deep, ROUND, 2 * seqs, LEN), BF16),
        pltpu.VMEM((ROUND, deep, HEAD // 2, LEN), BF16),
        pltpu.VMEM((ROUND, deep, HEAD // 2, LEN), BF16),
        pltpu.VMEM((deep, HEAD // 2, LEN), BF16),
        pltpu.VMEM((deep, HEAD // 2, LEN), BF16),
        pltpu.VMEM((HEAD // 2, LEN), BF16),
        pltpu.VMEM((seqs, HEAD // 2, LEN), BF16),
    ]
    band = (BAND + 1) * LEN
    work = [
        pltpu.VMEM((4 * WIDTH, LEN), F32),
        pltpu.VMEM((4 * WIDTH, LEN), F32),
        pltpu.VMEM((WIDTH, LEN), F32),
        pltpu.VMEM((WIDTH, LEN), F32),
        pltpu.VMEM((WIDTH, LEN), F32),
        pltpu.VMEM((group, HEAD), BF16),
        pltpu.VMEM((group, HEAD), BF16),
        pltpu.VMEM((seqs, band, LEN), BF16),
        pltpu.VMEM((seqs, band, LEN), F32),
        pltpu.VMEM((seqs, HEAD, LEN), F32),
        pltpu.VMEM((seqs, 2, HEAD, LEN), F32),
        pltpu.VMEM((4 * WIDTH, LEN), BF16),
        pltpu.VMEM((64 * tabs, group), BF16),
        pltpu.VMEM((chunks, LEN, LEN), BF16),
        pltpu.VMEM((chunks, seqs, 2 * seqs, WIDTH), BF16),
        pltpu.VMEM((512, chunks * LEN), BF16),
    ]
    dma = pltpu.SemaphoreType.DMA
    sems = [dma((13,)), dma((13,)), dma((seqs,))] + [dma((chunks,)) for _ in range(6)]

    def local(history_rows, out_grad, seg_lengths, hot_flag, hot_slot, cold_owner, cold_row, input_weight, w_out):
        vmem = pl.BlockSpec(memory_space=pltpu.VMEM)
        return pl.pallas_call(
            functools.partial(kernel, seqs, tabs),
            out_shape=(
                jax.ShapeDtypeStruct((512, WIDTH), F32),
                jax.ShapeDtypeStruct((64, WIDTH), F32),
            ),
            in_specs=[pl.BlockSpec(memory_space=pltpu.HBM)] * 9,
            out_specs=(vmem, vmem),
            scratch_shapes=inputs + exchanged + work + sems,
            compiler_params=pltpu.CompilerParams(
                collective_id=0, has_side_effects=True, vmem_limit_bytes=56 * 1024 * 1024
            ),
        )(
            history_rows.reshape(LEN, WIDTH),
            out_grad.reshape(LEN, WIDTH),
            seg_lengths,
            hot_flag,
            hot_slot,
            cold_owner.reshape(1, LEN),
            cold_row,
            input_weight,
            w_out,
        )

    in_specs = (
        P("tab", "seq", None),
        P("tab", "seq", None),
        P("tab", None),
        P("tab", "seq"),
        P("tab", "seq"),
        P("tab", "seq", None),
        P("tab", "seq"),
        P(),
        P(),
    )
    out_specs = (P(("seq", "tab"), None), P("tab", None))
    return jax.shard_map(local, mesh=mesh, in_specs=in_specs, out_specs=out_specs, check_vma=False)
```

```python
import functools

import jax
import jax.numpy as jnp
from jax import lax
from jax.experimental import pallas as pl
from jax.experimental.pallas import tpu as pltpu
from jax.sharding import PartitionSpec as P

HEADS = 8
HEAD = 64
LEN = 128
WIDTH = 512
BAND = 4
EPS = 1e-05
MESH = pl.DeviceIdType.MESH
F32 = jnp.float32
BF16 = jnp.bfloat16
I32 = jnp.int32
VALUE, QUERY, KEY = 0, 1, 2
ROUND = 4
NEAR = None


def mm(a, b):
    return jnp.dot(a, b, preferred_element_type=F32)


def mm_t(a, b):
    return lax.dot_general(a, b, (((1,), (1,)), ((), ())), preferred_element_type=F32)


def sigmoid(v):
    return 0.5 * jnp.tanh(0.5 * v) + 0.5


def iota(shape, dim):
    return lax.broadcasted_iota(I32, shape, dim)


def kernel(
    seqs, tabs,
    x_hbm, og_hbm, seg_hbm, flag_hbm, slot_hbm, owner_hbm, row_hbm, w_hbm, wo_hbm,
    cold_ref, hot_ref,
    x_ref, og_ref, seg_ref, flag_ref, slot_ref, owner_ref, row_ref, w_ref, wo_ref, in_sem,
    qkv_send, qkv_recv, n_send, n_recv, id_send, id_recv, stat_send, stat_recv, off_send, off_recv, dg_send, dg_recv,
    row_send, row_recv, near_send, near_recv, tab_send, tab_recv, far_send, far_recv, numy_send, numy_recv, numz_recv,
    hoty_send, hoty_recv, hotz_send, hotz_recv, sum_send, sum_recv,
    proj, slope_in, xhat, straight, gated, keys, values, weight, slope, att, dkv, gproj, hits, own_hits, packed, table,
    send_sem, recv_sem, qkv_rs, cold_ss, cold_rs, tab_ss, tab_rs, far_ss, far_rs,
):
    me = lax.axis_index("seq")
    tab = lax.axis_index("tab")
    deep = tabs // ROUND
    z, y = tab // ROUND, lax.rem(tab, ROUND)
    chunks = deep // 2
    last = chunks - 1
    near = NEAR if NEAR is not None else chunks // 2
    lanes = 2 * ROUND
    share = 64

    def far_z(chunk, side):
        if isinstance(chunk, int):
            return deep // 2 * (1 - side) if chunk == last else (chunk + 1) * (1 - 2 * side)
        return jnp.where(chunk == last, deep // 2 * (1 - side), (chunk + 1) * (1 - 2 * side))

    def tab_peer(chunk, lane):
        return lax.rem(z + far_z(chunk, lane // ROUND) + deep, deep) * ROUND + lax.rem(lane, ROUND)

    def tab_slot(chunk, lane):
        side = lane // ROUND
        return chunk * lanes + (side if chunk == last else 1 - side) * ROUND + y

    def remote(src, dst, ss, rs, peer):
        return pltpu.make_async_remote_copy(
            src_ref=src, dst_ref=dst, send_sem=ss, recv_sem=rs, device_id=peer, device_id_type=MESH
        )

    begun = []

    class Exchange:
        def __init__(self, ss, rs, sizing):
            self.ss, self.rs, self.sizing = ss, rs, sizing
            self.left = {"sent", "got"}

        def start(self, src, dst, axis, peer):
            if self not in begun:
                begun.append(self)
            remote(src, dst, self.ss, self.rs, {axis: peer}).start()

        def sent(self):
            self.left.discard("sent")
            remote(self.sizing, self.sizing, self.ss, self.rs, {"seq": me}).wait_send()

        def got(self):
            self.left.discard("got")
            remote(self.sizing, self.sizing, self.ss, self.rs, {"seq": me}).wait_recv()

    def finish():
        for one in begun:
            for name in sorted(one.left):
                getattr(one, name)()

    def seq_all(exchange, out, into):
        for step in range(1, seqs):
            peer = lax.rem(me + step, seqs)
            exchange.start(out(peer), into, "seq", peer)

    def tab_chunk(exchange, chunk, out, into):
        def one(lane):
            exchange.start(out(lane), into.at[tab_slot(chunk, lane)], "tab", tab_peer(chunk, lane))

        if chunk == last:
            pl.loop(0, ROUND)(one)

            @pl.loop(1, ROUND)
            def _(step):
                one(ROUND + lax.rem(y + step, ROUND))
        else:
            pl.loop(0, lanes)(one)

    home = last * lanes + ROUND + y

    def tab_sizing(into, chunk):
        return into.at[pl.ds(chunk * lanes, lanes - 1 if chunk == last else lanes)]

    others = pl.ds(0, seqs - 1)
    ns = Exchange(send_sem.at[1], recv_sem.at[1], n_recv.at[others])
    ids = Exchange(send_sem.at[2], recv_sem.at[2], id_recv.at[others])
    stats = [Exchange(send_sem.at[3 + half], recv_sem.at[3 + half], stat_recv.at[half, others]) for half in range(2)]
    offs = Exchange(send_sem.at[5], recv_sem.at[5], off_recv.at[others])
    dg = Exchange(send_sem.at[6], recv_sem.at[6], dg_recv.at[others])
    row = Exchange(send_sem.at[7], recv_sem.at[7], row_recv.at[others])
    numy = Exchange(send_sem.at[8], recv_sem.at[8], numy_recv.at[pl.ds(0, ROUND - 1)])
    numz = Exchange(send_sem.at[9], recv_sem.at[9], numz_recv.at[pl.ds(0, deep - 1)])
    hoty = Exchange(send_sem.at[10], recv_sem.at[10], hoty_recv.at[pl.ds(0, ROUND - 1)])
    hotz = Exchange(send_sem.at[11], recv_sem.at[11], hotz_recv.at[pl.ds(0, deep - 1)])
    total = Exchange(send_sem.at[12], recv_sem.at[12], sum_recv.at[others])
    cold = Exchange(cold_ss.at[0], cold_rs.at[0], near_recv.at[others])
    along = [Exchange(tab_ss.at[c], tab_rs.at[c], tab_sizing(tab_recv, c)) for c in range(chunks)]
    back = [Exchange(far_ss.at[c], far_rs.at[c], far_recv.at[c, others]) for c in range(chunks - near)]

    loads = [
        pltpu.make_async_copy(src, dst, in_sem.at[index])
        for index, (src, dst) in enumerate(
            (
                (flag_hbm, flag_ref),
                (slot_hbm, slot_ref),
                (owner_hbm, owner_ref),
                (row_hbm, row_ref),
                (x_hbm, x_ref),
                (w_hbm.at[:, pl.ds(WIDTH, 3 * WIDTH)], w_ref.at[:, pl.ds(WIDTH, 3 * WIDTH)]),
                (seg_hbm, seg_ref),
                (og_hbm, og_ref),
                (wo_hbm, wo_ref),
                (w_hbm.at[:, pl.ds(0, WIDTH)], w_ref.at[:, pl.ds(0, WIDTH)]),
            )
        )
    ]
    for load in loads:
        load.start()

    barrier = pltpu.get_barrier_semaphore()
    for step in range(1, seqs):
        pl.semaphore_signal(barrier, inc=1, device_id={"seq": lax.rem(me + step, seqs)}, device_id_type=MESH)

    for step in range(1, ROUND):
        peer = z * ROUND + lax.rem(y + step, ROUND)
        pl.semaphore_signal(barrier, inc=1, device_id={"tab": peer}, device_id_type=MESH)
    for step in range(1, deep):
        peer = lax.rem(z + step, deep) * ROUND + y
        pl.semaphore_signal(barrier, inc=1, device_id={"tab": peer}, device_id_type=MESH)

    for load in loads[:4]:
        load.wait()
    flag = flag_ref[...]
    owner = jnp.where(flag == 1, -1, owner_ref[...])
    owner_row = jnp.broadcast_to(owner.astype(F32), (LEN, LEN))
    earlier = (owner_row.T == owner_row) & (iota((LEN, LEN), 0) < iota((LEN, LEN), 1))
    taken = jnp.sum(jnp.where(earlier, 1.0, 0.0), axis=0, keepdims=True)
    lane_of = jnp.where(flag == 1, -1, owner * 2 + taken.astype(I32))
    which = iota((8, LEN), 0)
    id_send[...] = jnp.where(
        which == 0,
        jnp.where(flag == 1, slot_ref[...], -1),
        jnp.where(which == 1, lane_of, jnp.where(which == 2, row_ref[...], 0)),
    )
    id_recv[me] = id_send[...]

    loads[4].wait()
    wide = x_ref[...].astype(F32)
    centered = wide - jnp.mean(wide, axis=1, keepdims=True)
    normed = centered * lax.rsqrt(jnp.mean(centered * centered, axis=1, keepdims=True) + EPS)
    xin = normed.astype(BF16)

    def project(block, pair):
        spot = pl.multiple_of(block * WIDTH + pair * LEN, LEN)
        out = mm(xin, w_ref[:, pl.ds(spot, LEN)]).T
        proj[pl.ds(spot, LEN), :] = out
        return (out * sigmoid(out)).astype(BF16).reshape(2, HEAD, LEN)

    def qkv_copy(peer):
        return remote(qkv_send.at[peer], qkv_recv.at[me], send_sem.at[0], qkv_rs.at[me], {"seq": peer})

    loads[5].wait()
    pairs = [lax.rem(me // 2 + 1 + step, HEADS // 2) for step in range(HEADS // 2)]
    for pair in pairs:
        for part, block in ((VALUE, 1), (QUERY, 2), (KEY, 3)):
            qkv_send[pl.ds(2 * pair, 2), part] = project(block, pair)
    pl.semaphore_wait(barrier, seqs - 1 + ROUND - 1 + deep - 1)
    for pair in pairs:
        for core in range(2):
            peer = 2 * pair + core

            @pl.when(peer != me)
            def _():
                qkv_copy(peer).start()

    qkv_recv[me] = qkv_send[me]

    for load in loads[6:]:
        load.wait()
    for pair in pairs:
        spot = pl.multiple_of(pair * LEN, LEN)
        up = mm_t(wo_ref[pl.ds(spot, LEN), :], og_ref[...])
        gated[pl.ds(spot, LEN), :] = up
        n_send[pl.ds(2 * pair, 2)] = (up.reshape(2, HEAD, LEN) * project(0, pair).astype(F32)).astype(BF16)
    n_recv[me] = n_send[me]

    for chunk in range(chunks):
        place = iota((lanes * 2 * seqs, LEN), 0)
        major, minor = place >> 4, (place >> 1) & 7
        to_seq, lane = (major, minor) if chunk < near else (minor, major)
        wanted = (to_seq * tabs + tab_peer(chunk, lane)) * 2 + (place & 1)
        own_hits[chunk] = jnp.where(wanted == id_send[1:2, :], 1.0, 0.0).astype(BF16)

    end0 = seg_ref[0, 0]
    end1 = end0 + seg_ref[0, 1]
    end2 = end1 + seg_ref[0, 2]
    for step in range(HEADS // 2):
        for core in range(2):
            source = 2 * lax.rem(me // 2 + 3 - step + HEADS // 2, HEADS // 2) + core

            @pl.when(source != me)
            def _():
                slab = qkv_recv.at[source]
                remote(slab, slab, send_sem.at[0], qkv_rs.at[source], {"seq": me}).wait_recv()

            span = pl.ds(pl.multiple_of(source * LEN, LEN), LEN)
            keys[span, :] = qkv_recv[source, KEY].astype(F32).T.astype(BF16)
            values[span, :] = qkv_recv[source, VALUE].astype(F32).T.astype(BF16)
        if step == 0:
            seq_all(ns, lambda peer: n_send.at[peer], n_recv.at[me])
            seq_all(ids, lambda peer: id_send, id_recv.at[me])

    half = seqs // 2
    for block in reversed(range(seqs)):
        low = max(0, block - BAND)
        count = block + 1 - low
        score = mm(keys[pl.ds(low * LEN, count * LEN), :], qkv_recv[block, QUERY]) * 0.125
        here = block * LEN + iota((1, LEN), 1)
        start = jnp.where(here >= end2, end2, jnp.where(here >= end1, end1, jnp.where(here >= end0, end0, 0)))
        there = low * LEN + iota(score.shape, 0)
        allowed = (there >= start) & (there <= here)
        gate = sigmoid(score)
        swish = score * gate
        heavy = jnp.where(allowed, swish, 0.0).astype(BF16)
        weight[block, pl.ds(0, count * LEN), :] = heavy
        slope[block, pl.ds(0, count * LEN), :] = jnp.where(allowed, (gate + swish * (1.0 - gate)) * 0.125, 0.0)
        across = jnp.concatenate([qkv_recv[other, VALUE] for other in range(low, block + 1)], axis=1)
        mixed = mm(across, heavy)
        if block == seqs - 1:
            ns.got()
        grad = n_recv[block].astype(F32)
        mean = jnp.mean(mixed, axis=0, keepdims=True)
        off = mixed - mean
        att[block] = off
        off_send[block] = off.astype(BF16)
        part, line = block // half, block % half
        for kind, sums in enumerate(
            (
                mean,
                jnp.sum(off * off, axis=0, keepdims=True),
                jnp.sum(grad, axis=0, keepdims=True),
                jnp.sum(grad * off, axis=0, keepdims=True),
            )
        ):
            stat_send[part, pl.ds(kind * half + line, 1), :] = sums
        if line == 0:
            seq_all(stats[part], lambda peer: stat_send.at[part], stat_recv.at[part, me])
            stat_recv[part, me] = stat_send[part]
    seq_all(offs, lambda peer: off_send.at[peer], off_recv.at[me])
    off_recv[me] = off_send[me]

    ids.got()
    place = iota((LEN, LEN), 0)
    for step in range(ROUND):
        peer = lax.rem(y + 1 + step, ROUND)
        wanted = (me * tabs + (place >> 4) * ROUND + peer) * 2 + (place & 1)
        numbers = jnp.zeros((2 * seqs, LEN), F32)
        for source in range(seqs):
            mine = jnp.where(((place >> 1) & (seqs - 1)) == source, wanted, -5)
            pick = jnp.where(mine == id_recv[source, 1:2, :], 1.0, 0.0).astype(BF16)
            number = id_recv[source, 2:3, :]
            line = iota((2 * seqs, LEN), 0)
            halves = jnp.where(line == 0, number >> 4, jnp.where(line == 1, number & 15, 0))
            numbers = numbers + mm_t(halves.astype(F32).astype(BF16), pick)
        numy_send[peer] = numbers.astype(BF16)
        if step < ROUND - 1:
            numy.start(numy_send.at[peer], numy_recv.at[y], "tab", z * ROUND + peer)
    numy_recv[y] = numy_send[y]

    across = x_ref[...].astype(F32).T
    across = across - jnp.mean(across, axis=0, keepdims=True)
    inv_in = lax.rsqrt(jnp.mean(across * across, axis=0, keepdims=True) + EPS)
    xhat[...] = across * inv_in
    straight[...] = og_ref[...].astype(F32).T

    @pl.loop(0, 4)
    def _(block):
        span = pl.ds(pl.multiple_of(block * WIDTH, WIDTH), WIDTH)
        value = proj[span, :]
        gate = sigmoid(value)
        slope_in[span, :] = gate * (1.0 + value * (1.0 - gate))

    hot_ids = jnp.concatenate([id_recv[source, 0:1, :] for source in range(seqs)], axis=1)
    to_y, to_z = (hot_ids >> 6) & (ROUND - 1), hot_ids >> 8
    hot_ids = jnp.where(hot_ids < 0, -1, ((to_y * deep + to_z) << 6) | (hot_ids & 63))

    def hot_table(block):
        spot = pl.multiple_of(block * LEN, LEN)
        hits[pl.ds(spot, LEN), :] = jnp.where(iota((LEN, seqs * LEN), 0) + spot == hot_ids, 1.0, 0.0).astype(BF16)

    tables = hits.shape[0] // LEN
    pl.loop(0, tables // 2)(hot_table)
    ids.sent()
    ns.sent()
    remote(qkv_recv.at[others], qkv_recv.at[others], send_sem.at[0], qkv_rs.at[0], {"seq": me}).wait_send()

    def pooled(mean_of, spread_of, first_of, second_of):
        mean = sum(mean_of) * (1.0 / seqs)
        spread = sum(spread_of[head] + HEAD * (mean_of[head] - mean) ** 2 for head in range(seqs))
        inv = lax.rsqrt(spread * (1.0 / WIDTH) + EPS)
        first = sum(first_of) * (1.0 / WIDTH)
        second = sum(second_of[head] + (mean_of[head] - mean) * first_of[head] for head in range(seqs))
        return mean, inv, first, inv * second * (1.0 / WIDTH)

    def norms(part):
        stats[part].got()
        sums = [[stat_recv[part, head, pl.ds(kind * half, half), :] for head in range(seqs)] for kind in range(4)]
        own_mean = stat_send[part, pl.ds(0, half), :]
        return (own_mean,) + pooled(*sums)

    for block in reversed(range(seqs)):
        low = max(0, block - BAND)
        count = block + 1 - low
        if block % half == half - 1:
            norm = norms(block // half)
        own_mean, mean, inv, first, second = (array[block % half : block % half + 1, :] for array in norm)
        normed_here = (att[block] + (own_mean - mean)) * inv
        grad = (inv * (n_recv[block].astype(F32) - first - normed_here * second)).astype(BF16)
        query = qkv_recv[block, QUERY]
        span = pl.ds(low * LEN, count * LEN)
        grad_weight = mm(values[span, :], grad)
        grad_score = (grad_weight * slope[block, pl.ds(0, count * LEN), :]).astype(BF16)
        across = jnp.concatenate([qkv_recv[other, KEY] for other in range(low, block + 1)], axis=1)
        grad_value = mm_t(grad, weight[block, pl.ds(0, count * LEN), :])
        grad_key = mm_t(query, grad_score)
        dg_send[block, QUERY] = mm(across, grad_score).astype(BF16)
        for other in range(low, block + 1):
            cut = slice((other - low) * LEN, (other - low + 1) * LEN)
            new_value, new_key = grad_value[:, cut], grad_key[:, cut]
            if block < min(seqs - 1, other + BAND):
                new_value, new_key = new_value + dkv[other, 0], new_key + dkv[other, 1]
            if other == block:
                dg_send[block, VALUE] = new_value.astype(BF16)
                dg_send[block, KEY] = new_key.astype(BF16)
            else:
                dkv[other, 0] = new_value
                dkv[other, 1] = new_key

        @pl.when(block != me)
        def _():
            dg.start(dg_send.at[block], dg_recv.at[me], "seq", block)

    dg_recv[me] = dg_send[me]

    numy.got()
    for step in range(1, deep):
        peer = lax.rem(z + step, deep)
        numz.start(numy_recv, numz_recv.at[z], "tab", peer * ROUND + y)
    numz_recv[z] = numy_recv[...]

    pl.loop(tables // 2, tables)(hot_table)
    out_at, in_at = iota((LEN, LEN), 0), iota((LEN, LEN), 1)
    order = jnp.where(
        ((out_at >> 4) == ((in_at >> 1) & 7)) & (((out_at >> 1) & 7) == (in_at >> 4)) & ((out_at & 1) == (in_at & 1)), 1.0, 0.0
    ).astype(BF16)
    offs.got()
    sums = []
    for kind in range(4):
        spot = kind * half + lax.rem(me, half)
        sums.append([stat_recv[me // half, head, pl.ds(spot, 1), :] for head in range(seqs)])
    mean, inv, _, _ = pooled(*sums)
    for head in range(HEADS):
        span = pl.ds(head * HEAD, HEAD)
        normed_here = (off_recv[head].astype(F32) + (sums[0][head] - mean)) * inv
        gproj[span, :] = (gated[span, :] * normed_here * slope_in[span, :]).astype(BF16)
    grad_in = mm(w_ref[:, 0:WIDTH], gproj[0:WIDTH, :])
    for part in stats:
        part.sent()
    offs.sent()
    numy.sent()

    dg.got()
    for part in range(3):
        span = pl.ds((part + 1) * WIDTH, WIDTH)
        gproj[span, :] = (dg_recv[:, part].reshape(WIDTH, LEN).astype(F32) * slope_in[span, :]).astype(BF16)
    grad_in = grad_in + mm(w_ref[:, WIDTH:], gproj[WIDTH:, :])
    norm_in = xhat[...]
    grad_rows = straight[...] + inv_in * (
        grad_in
        - jnp.mean(grad_in, axis=0, keepdims=True)
        - norm_in * jnp.mean(grad_in * norm_in, axis=0, keepdims=True)
    )
    grad_rows = grad_rows.astype(BF16)

    row_send[...] = grad_rows.reshape(row_send.shape)
    seq_all(row, lambda peer: row_send.at[peer], row_recv.at[me])
    row_recv[me] = row_send[me]

    for chunk in reversed(range(near, chunks)):
        packed[chunk] = mm_t(own_hits[chunk], grad_rows).astype(BF16).reshape(seqs, 2 * seqs, WIDTH)
        tab_chunk(along[chunk], chunk, lambda lane: packed.at[chunk, lane], tab_recv)
        if chunk == last:
            tab_recv[home] = packed[chunk, ROUND + y]
    for chunk in range(near):
        packed[chunk] = mm_t(own_hits[chunk], grad_rows).astype(BF16).reshape(seqs, 2 * seqs, WIDTH)
        for peer in range(seqs):
            near_send[peer, chunk] = packed[chunk, peer]
    if near:
        seq_all(cold, lambda peer: near_send.at[peer], near_recv.at[me])
        near_recv[me] = near_send[me]
    dg.sent()

    numz.got()
    for chunk in range(chunks):
        numbers = jnp.zeros((8, LEN), F32)
        lane_at = iota((8, LEN), 1) >> 4
        for lane in range(lanes):
            source = lax.rem(z + far_z(chunk, lane // ROUND) + deep, deep)
            tile = numz_recv[source, lane % ROUND].astype(F32)[:8]
            shift = lax.rem(2 * seqs * (lane - z) + LEN, LEN)
            numbers = jnp.where(lane_at == lane, pltpu.roll(tile, shift, 1), numbers)
        if chunk >= near:
            numbers = mm_t(numbers.astype(BF16), order)
        numbers = (16.0 * numbers[0:1, :] + numbers[1:2, :]).astype(I32)
        table[:, pl.ds(chunk * LEN, LEN)] = jnp.where(iota((cold_ref.shape[0], LEN), 0) == numbers, 1.0, 0.0).astype(BF16)
    numz.sent()

    row.got()
    slab = jnp.concatenate([row_recv[source] for source in range(seqs)], axis=1)
    slab = jnp.concatenate([slab, slab], axis=0)
    left = iota((share // 2, LEN), 1) < HEAD
    for step in range(ROUND):
        peer = lax.rem(y + 1 + step, ROUND)
        sums = mm_t(hits[pl.ds(pl.multiple_of(peer * deep * share, deep * share), deep * share), :], slab)
        for plane in range(deep):
            first = plane * share
            upper, lower = sums[first : first + share // 2], sums[first + share // 2 : first + share]
            hoty_send[peer, plane] = jnp.where(left, upper, lower).astype(BF16)
        if step < ROUND - 1:
            hoty.start(hoty_send.at[peer], hoty_recv.at[y], "tab", z * ROUND + peer)
    hoty_recv[y] = hoty_send[y]

    if near:
        cold.got()
    for chunk in reversed(range(near)):
        rows = mm(order, near_recv[:, chunk].reshape(LEN, WIDTH)).astype(BF16)
        tab_send[chunk] = rows.reshape(lanes, 2 * seqs, WIDTH)
        tab_chunk(along[chunk], chunk, lambda lane: tab_send.at[chunk, lane], tab_recv)
        if chunk == last:
            tab_recv[home] = tab_send[chunk, ROUND + y]

    hoty.got()
    for plane in range(deep):
        sums = sum(hoty_recv[source, plane].astype(F32) for source in range(ROUND))
        hotz_send[plane] = sums.astype(BF16)
    for step in range(1, deep):
        peer = lax.rem(z + step, deep)
        hotz.start(hotz_send.at[peer], hotz_recv.at[z], "tab", peer * ROUND + y)
    hotz_recv[z] = hotz_send[z]

    for chunk in reversed(range(near, chunks)):
        along[chunk].got()
        rows = mm(order, tab_recv[pl.ds(chunk * lanes, lanes)].reshape(LEN, WIDTH)).astype(BF16)
        far_send[chunk - near] = rows.reshape(seqs, 2 * lanes, WIDTH)
        seq_all(back[chunk - near], lambda peer: far_send.at[chunk - near, peer], far_recv.at[chunk - near, me])
        far_recv[chunk - near, me] = far_send[chunk - near, me]

    hotz.got()
    sum_send[...] = sum(hotz_recv[source].astype(F32) for source in range(deep)).astype(BF16)
    seq_all(total, lambda peer: sum_send, sum_recv.at[me])
    sum_recv[me] = sum_send[...]
    row.sent()
    hoty.sent()
    hotz.sent()
    if near:
        cold.sent()
    for chunk in range(near, chunks):
        along[chunk].sent()

    for chunk in range(near):
        along[chunk].got()
    result = jnp.zeros(cold_ref.shape, F32)
    if near:
        result = mm(table[:, : near * LEN], tab_recv[0 : near * lanes].reshape(near * LEN, WIDTH))
    for part in back:
        part.got()
    if near < chunks:
        result = result + mm(table[:, near * LEN :], far_recv[...].reshape((chunks - near) * LEN, WIDTH))
    cold_ref[...] = result

    total.got()
    for pair in range(seqs // 2):
        even, odd = sum_recv[2 * pair].astype(F32), sum_recv[2 * pair + 1].astype(F32)
        span = pl.ds(pair * LEN, LEN)
        hot_ref[0 : share // 2, span] = jnp.where(left, even, pltpu.roll(odd, HEAD, 1))
        hot_ref[share // 2 :, span] = jnp.where(left, pltpu.roll(even, HEAD, 1), odd)

    finish()


def write_out(cold_ref, hot_ref, cold_out, hot_out, sems):
    copies = [
        pltpu.make_async_copy(src, dst, sems.at[index])
        for index, (src, dst) in enumerate(((cold_ref, cold_out), (hot_ref, hot_out)))
    ]
    for copy in copies:
        copy.start()
    for copy in copies:
        copy.wait()


def solution(mesh):
    seqs, tabs = mesh.shape["seq"], mesh.shape["tab"]
    deep = tabs // ROUND
    chunks = deep // 2
    near = NEAR if NEAR is not None else chunks // 2
    lanes = 2 * ROUND
    group = seqs * LEN
    inputs = [
        pltpu.VMEM((LEN, WIDTH), BF16),
        pltpu.VMEM((LEN, WIDTH), BF16),
        pltpu.SMEM((1, 4), I32),
        pltpu.VMEM((1, LEN), I32),
        pltpu.VMEM((1, LEN), I32),
        pltpu.VMEM((1, LEN), I32),
        pltpu.VMEM((1, LEN), I32),
        pltpu.VMEM((WIDTH, 4 * WIDTH), BF16),
        pltpu.VMEM((WIDTH, WIDTH), BF16),
        pltpu.SemaphoreType.DMA((10,)),
    ]
    exchanged = [
        pltpu.VMEM((HEADS, 3, HEAD, LEN), BF16),
        pltpu.VMEM((seqs, 3, HEAD, LEN), BF16),
        pltpu.VMEM((HEADS, HEAD, LEN), BF16),
        pltpu.VMEM((seqs, HEAD, LEN), BF16),
        pltpu.VMEM((8, LEN), I32),
        pltpu.VMEM((seqs, 8, LEN), I32),
        pltpu.VMEM((2, 2 * seqs, LEN), F32),
        pltpu.VMEM((2, seqs, 2 * seqs, LEN), F32),
        pltpu.VMEM((seqs, HEAD, LEN), BF16),
        pltpu.VMEM((HEADS, HEAD, LEN), BF16),
        pltpu.VMEM((seqs, 3, HEAD, LEN), BF16),
        pltpu.VMEM((HEADS, 3, HEAD, LEN), BF16),
        pltpu.VMEM((seqs, HEAD, LEN), BF16),
        pltpu.VMEM((seqs, HEAD, LEN), BF16),
        pltpu.VMEM((seqs, max(near, 1), 2 * lanes, WIDTH), BF16),
        pltpu.VMEM((seqs, max(near, 1), 2 * lanes, WIDTH), BF16),
        pltpu.VMEM((max(near, 1), lanes, 2 * seqs, WIDTH), BF16),
        pltpu.VMEM((tabs, 2 * seqs, WIDTH), BF16),
        pltpu.VMEM((max(chunks - near, 1), seqs, 2 * lanes, WIDTH), BF16),
        pltpu.VMEM((max(chunks - near, 1), seqs, 2 * lanes, WIDTH), BF16),
        pltpu.VMEM((ROUND, 2 * seqs, LEN), BF16),
        pltpu.VMEM((ROUND, 2 * seqs, LEN), BF16),
        pltpu.VMEM((deep, ROUND, 2 * seqs, LEN), BF16),
        pltpu.VMEM((ROUND, deep, HEAD // 2, LEN), BF16),
        pltpu.VMEM((ROUND, deep, HEAD // 2, LEN), BF16),
        pltpu.VMEM((deep, HEAD // 2, LEN), BF16),
        pltpu.VMEM((deep, HEAD // 2, LEN), BF16),
        pltpu.VMEM((HEAD // 2, LEN), BF16),
        pltpu.VMEM((seqs, HEAD // 2, LEN), BF16),
    ]
    band = (BAND + 1) * LEN
    work = [
        pltpu.VMEM((4 * WIDTH, LEN), F32),
        pltpu.VMEM((4 * WIDTH, LEN), F32),
        pltpu.VMEM((WIDTH, LEN), F32),
        pltpu.VMEM((WIDTH, LEN), F32),
        pltpu.VMEM((WIDTH, LEN), F32),
        pltpu.VMEM((group, HEAD), BF16),
        pltpu.VMEM((group, HEAD), BF16),
        pltpu.VMEM((seqs, band, LEN), BF16),
        pltpu.VMEM((seqs, band, LEN), F32),
        pltpu.VMEM((seqs, HEAD, LEN), F32),
        pltpu.VMEM((seqs, 2, HEAD, LEN), F32),
        pltpu.VMEM((4 * WIDTH, LEN), BF16),
        pltpu.VMEM((64 * tabs, group), BF16),
        pltpu.VMEM((chunks, LEN, LEN), BF16),
        pltpu.VMEM((chunks, seqs, 2 * seqs, WIDTH), BF16),
        pltpu.VMEM((512, chunks * LEN), BF16),
    ]
    dma = pltpu.SemaphoreType.DMA
    sems = [dma((13,)), dma((13,)), dma((seqs,))] + [dma((chunks,)) for _ in range(6)]

    def local(history_rows, out_grad, seg_lengths, hot_flag, hot_slot, cold_owner, cold_row, input_weight, w_out):
        vmem = pl.BlockSpec(memory_space=pltpu.VMEM)
        cold, hot = pl.pallas_call(
            functools.partial(kernel, seqs, tabs),
            out_shape=(
                jax.ShapeDtypeStruct((512, WIDTH), F32),
                jax.ShapeDtypeStruct((64, WIDTH), F32),
            ),
            in_specs=[pl.BlockSpec(memory_space=pltpu.HBM)] * 9,
            out_specs=(vmem, vmem),
            scratch_shapes=inputs + exchanged + work + sems,
            compiler_params=pltpu.CompilerParams(
                collective_id=0, has_side_effects=True, vmem_limit_bytes=56 * 1024 * 1024
            ),
        )(
            history_rows.reshape(LEN, WIDTH),
            out_grad.reshape(LEN, WIDTH),
            seg_lengths,
            hot_flag,
            hot_slot,
            cold_owner.reshape(1, LEN),
            cold_row,
            input_weight,
            w_out,
        )
        return pl.pallas_call(
            write_out,
            out_shape=(jax.ShapeDtypeStruct(cold.shape, F32), jax.ShapeDtypeStruct(hot.shape, F32)),
            in_specs=[vmem, vmem],
            out_specs=(pl.BlockSpec(memory_space=pltpu.HBM),) * 2,
            scratch_shapes=[pltpu.SemaphoreType.DMA((2,))],
        )(cold, hot)

    in_specs = (
        P("tab", "seq", None),
        P("tab", "seq", None),
        P("tab", None),
        P("tab", "seq"),
        P("tab", "seq"),
        P("tab", "seq", None),
        P("tab", "seq"),
        P(),
        P(),
    )
    out_specs = (P(("seq", "tab"), None), P("tab", None))
    return jax.shard_map(local, mesh=mesh, in_specs=in_specs, out_specs=out_specs, check_vma=False)
```
